32 devices in a mesh: lat: 4 (over z), lon: 8 (over y, x, core).
Axes of the slice: x: 2, y: 2, z: 4, core: 2. Of those that a mesh axis runs over, the one named last changes fastest.
Arguments:
- grid_tokens: bfloat16 [96, 384, 512], P('lat', 'lon'), may hold values from -28 to 28
- attention_gain: float32 [512], replicated, may hold values from 0.25 to 1.75
- score_weight: bfloat16 [512, 1024], replicated, as said below
- value_weight: bfloat16 [512, 512], replicated, may hold values from -0.25 to 0.25
- output_weight: bfloat16 [512, 512], replicated, may hold values from -0.75 to 0.75
- mixer_gain: float32 [512], replicated, may hold values from 0.25 to 1.75
- first_weight: float32 [2, 8, 64, 64], replicated, may hold values from -0.5 to 0.5
- first_bias: float32 [2, 8, 64], replicated, may hold values from -0.75 to 0.75
- second_weight: float32 [2, 8, 64, 64], replicated, may hold values from -0.5 to 0.5
- second_bias: float32 [2, 8, 64], replicated, may hold values from -0.875 to 0.875
Outputs:
- block_out: bfloat16 [96, 384, 512], P('lat', 'lon')
The draws below stay inside these ranges and needn't reach their ends.
Inputs may be any that keep to these rules, and one draw needn't show every extreme that they name: `score_weight`: every entry lies within 61 / sqrt(512) of zero.
All inputs are finite; a program needn't handle non-finite values.
Results may differ from the reference program's by a relative error of at most 0.0095.
The reference program's roundings to bfloat16 on the way count: a program that leaves them out, or rounds other values in their place, can miss the bound.
Values may be sent and summed in bfloat16 or wider, within the bound.
A program may use at most 192 MiB of HBM per device.

```python
import math
import jax
import jax.numpy as jnp
from jax import lax

D = 512
HEADS = 8
HD = 64
NB = 8
BS = 64
RADIUS = 6
NH = 96
NW = 384
KQ = 24
KH = 48
MW = 96


def draw_grid_tokens(key, part):
    base_key = jax.random.fold_in(key, 0)
    field = jnp.clip(jax.random.normal(base_key, (NH, NW, D), jnp.float32), -6.0, 6.0)
    return field.astype(jnp.bfloat16)


def draw_score_weight(key, part):
    query_key, key_key = jax.random.split(key, 2)
    factor = 1.0 / math.sqrt(D)
    query_part = jnp.clip(jax.random.normal(query_key, (D, D), jnp.float32), -6.0, 6.0) * factor
    second = jnp.clip(jax.random.normal(key_key, (D, D), jnp.float32), -6.0, 6.0) * factor
    return jnp.concatenate([query_part, second], axis=1).astype(jnp.bfloat16)


def normal_values(stream_key, shape, deviation, limit, kind=jnp.bfloat16):
    entries = jax.random.normal(stream_key, shape, jnp.float32) * deviation
    return jnp.minimum(jnp.maximum(entries, -limit), limit).astype(kind)


def setup_inputs(seed: int = 0) -> dict:
    seeds = jax.random.split(jax.random.key(seed), 11)
    grid_tokens = draw_grid_tokens(jax.random.fold_in(seeds[10], 71), 0)
    attention_gain = jnp.clip(1.0 + 0.15 * jax.random.normal(seeds[1], (D,), jnp.float32), 0.25, 1.75)
    score_weight = draw_score_weight(jax.random.fold_in(seeds[10], 71), 0)
    value_weight = normal_values(seeds[3], (D, D), D ** -0.5, 0.25)
    output_weight = normal_values(seeds[4], (D, D), (D // 8) ** -0.5, 0.75)
    mixer_gain = jnp.clip(1.0 + 0.15 * jax.random.normal(seeds[5], (D,), jnp.float32), 0.25, 1.75)
    first_weight = normal_values(seeds[6], (2, NB, BS, BS), (2 * BS) ** -0.5, 0.5, jnp.float32)
    first_bias = normal_values(seeds[7], (2, NB, BS), 0.05, 0.75, jnp.float32)
    second_weight = normal_values(seeds[8], (2, NB, BS, BS), (2 * BS) ** -0.5, 0.5, jnp.float32)
    second_bias = normal_values(seeds[9], (2, NB, BS), 0.06, 0.875, jnp.float32)
    return dict(grid_tokens=grid_tokens, attention_gain=attention_gain, score_weight=score_weight, value_weight=value_weight, output_weight=output_weight, mixer_gain=mixer_gain, first_weight=first_weight, first_bias=first_bias, second_weight=second_weight, second_bias=second_bias)


HIGHEST = lax.Precision.HIGHEST

def normed(values, gain):
    data = values.astype(jnp.float32)
    centre = lax.optimization_barrier(jnp.mean(data, axis=-1, keepdims=True))
    centred = data - centre
    spread = lax.optimization_barrier(jnp.mean(centred * centred, axis=-1, keepdims=True))
    return (centred * lax.rsqrt(spread + 1e-05) * gain).astype(jnp.bfloat16)

def windowed(stacked):
    queries = stacked[0].astype(jnp.float32)
    keys = stacked[1].astype(jnp.float32)
    values = stacked[2].astype(jnp.float32)
    span = 2 * RADIUS + 1
    first = jnp.clip(jnp.arange(NH, dtype=jnp.int32) - RADIUS, 0, NH - span)
    scores = []
    for down in range(span):
        key_rows = jnp.take(keys, first + down, axis=0)
        for across in range(span):
            shifted = jnp.roll(key_rows, RADIUS - across, axis=1)
            scores.append(lax.optimization_barrier(jnp.sum(queries * shifted, axis=-1)))
    scores = jnp.stack(scores) / math.sqrt(HD)
    largest = lax.optimization_barrier(jnp.max(scores, axis=0))
    weights = jnp.exp(scores - largest)
    rounded = lax.optimization_barrier((weights / lax.optimization_barrier(jnp.sum(weights, axis=0))).astype(jnp.bfloat16))
    probs = rounded.astype(jnp.float32)
    total = jnp.zeros_like(queries)
    for down in range(span):
        value_rows = jnp.take(values, first + down, axis=0)
        for across in range(span):
            shifted = jnp.roll(value_rows, RADIUS - across, axis=1)
            total = total + probs[down * span + across][:, :, None] * shifted
    return total

def split_heads(matrix):
    return jnp.transpose(matrix.reshape(NH, NW, HEADS, HD), (2, 0, 1, 3))

def block_mix(inputs, weight):
    return jnp.einsum('kmbi,bio->kmbo', inputs, weight, precision=HIGHEST)

def reference(grid_tokens, attention_gain, score_weight, value_weight, output_weight, mixer_gain, first_weight, first_bias, second_weight, second_bias):
    normed_in = normed(grid_tokens, attention_gain).reshape(NH * NW, D)
    queries = jnp.dot(normed_in, score_weight[:, :D], preferred_element_type=jnp.float32).astype(jnp.bfloat16)
    keys = jnp.dot(normed_in, score_weight[:, D:], preferred_element_type=jnp.float32).astype(jnp.bfloat16)
    values = jnp.dot(normed_in, value_weight, preferred_element_type=jnp.float32).astype(jnp.bfloat16)
    stacked = jnp.stack([split_heads(queries), split_heads(keys), split_heads(values)], axis=1)
    per_head = lax.map(windowed, stacked)
    attended = jnp.transpose(per_head, (1, 2, 0, 3)).reshape(NH * NW, D).astype(jnp.bfloat16)
    projected = jnp.dot(attended, output_weight, preferred_element_type=jnp.float32)
    after_attention = (grid_tokens.astype(jnp.float32).reshape(NH * NW, D) + projected).astype(jnp.bfloat16).reshape(NH, NW, D)
    mixer_in = normed(after_attention, mixer_gain)
    full = jnp.fft.rfft2(mixer_in.astype(jnp.float32), axes=(0, 1), norm='ortho')
    kept = jnp.concatenate([jnp.arange(KQ, dtype=jnp.int32), jnp.arange(NH - KQ, NH, dtype=jnp.int32)])
    part = full[kept, :MW]
    real_in = jnp.real(part).reshape(KH, MW, NB, BS)
    imag_in = jnp.imag(part).reshape(KH, MW, NB, BS)
    hidden_r = jax.nn.relu(block_mix(real_in, first_weight[0]) - block_mix(imag_in, first_weight[1]) + first_bias[0])
    hidden_i = jax.nn.relu(block_mix(imag_in, first_weight[0]) + block_mix(real_in, first_weight[1]) + first_bias[1])
    filtered_r = block_mix(hidden_r, second_weight[0]) - block_mix(hidden_i, second_weight[1]) + second_bias[0]
    filtered_i = block_mix(hidden_i, second_weight[0]) + block_mix(hidden_r, second_weight[1]) + second_bias[1]
    filtered = (filtered_r + 1j * filtered_i).reshape(KH, MW, D)
    placed = jnp.zeros((NH, NW // 2 + 1, D), filtered.dtype).at[kept, :MW].set(filtered)
    spectral = jnp.fft.irfft2(placed, s=(NH, NW), axes=(0, 1), norm='ortho').astype(jnp.bfloat16)
    summed = after_attention.astype(jnp.float32) + mixer_in.astype(jnp.float32) + spectral.astype(jnp.float32)
    return summed.astype(jnp.bfloat16)
```

```python
import functools
import math

import jax
import jax.numpy as jnp
import numpy as np
from jax import lax
from jax.experimental import pallas as pl
from jax.experimental.pallas import tpu as pltpu
from jax.sharding import PartitionSpec as P

HEADS = 8
RADIUS = 6


def padded_2(cells, sides, width):
    for axis, dim in sides:
        count = lax.axis_size(axis)
        head = lax.slice_in_dim(cells, 0, width, axis=dim)
        tail = lax.slice_in_dim(cells, cells.shape[dim] - width, cells.shape[dim], axis=dim)
        cells = jnp.concatenate(
            [
                lax.ppermute(tail, axis, [(i, (i + 1) % count) for i in range(count)]),
                cells,
                lax.ppermute(head, axis, [((i + 1) % count, i) for i in range(count)]),
            ],
            axis=dim,
        )
    return cells


def normed(values, gain):
    data = values.astype(jnp.float32)
    centre = jnp.mean(data, axis=-1, keepdims=True)
    centred = data - centre
    spread = jnp.mean(centred * centred, axis=-1, keepdims=True)
    return (centred * lax.rsqrt(spread + 1e-05) * gain).astype(jnp.bfloat16)


LANES = 128
CHUNKS = 3
MESH = pl.DeviceIdType.MESH


def mixer_tables(total_rows, total_cols, sources, slots):
    kept_rows = total_rows // 2
    kept_cols = total_cols // 4
    modes = kept_cols // sources
    column = np.arange(total_cols)
    angle = 2.0 * np.pi * (np.outer(np.arange(kept_cols), column) % total_cols) / total_cols
    cosine = np.cos(angle).reshape(sources, modes, total_cols)
    sine = np.sin(angle).reshape(sources, modes, total_cols)
    forward = np.zeros((sources, slots, total_cols))
    forward[:, 0 : 2 * modes : 2] = cosine
    forward[:, 1 : 2 * modes : 2] = -sine
    doubled = np.full((kept_cols, 1), 2.0)
    doubled[0] = 1.0
    inverse = (forward.reshape(sources, slots, total_cols)).copy()
    inverse[:, 0 : 2 * modes : 2] *= doubled.reshape(sources, modes, 1)
    inverse[:, 1 : 2 * modes : 2] *= doubled.reshape(sources, modes, 1)
    forward = forward.reshape(sources * slots, total_cols)
    inverse = inverse.reshape(sources * slots, total_cols).T
    frequency = np.arange(kept_rows)
    frequency = frequency + np.where(frequency >= kept_rows // 2, total_rows - kept_rows, 0)
    angle = 2.0 * np.pi * (np.outer(frequency, np.arange(total_rows)) % total_rows) / total_rows
    cosine = np.cos(angle)
    sine = np.sin(angle)
    lat_forward = np.block([[cosine, sine], [-sine, cosine]])
    lat_inverse = np.block([[cosine.T, -sine.T], [sine.T, cosine.T]])
    return tuple(
        np.asarray(table, dtype=jnp.bfloat16)
        for table in (forward, lat_forward, lat_inverse, inverse)
    )


def mixer_kernel(
    lat_count,
    lon_count,
    mixer_ref,
    forward_ref,
    lat_forward_ref,
    lat_inverse_ref,
    inverse_ref,
    weight_one_ref,
    bias_one_ref,
    weight_two_ref,
    bias_two_ref,
    out_ref,
    columns_in,
    modes_out,
    modes_in,
    modes_work,
    back_out,
    back_in,
    columns_out,
    lon_send,
    lon_recv,
    mode_send,
    mode_recv,
    back_send,
    back_recv,
    tile_send,
    tile_recv,
):
    tile_rows, tile_cols, features = mixer_ref.shape
    groups = features // LANES
    parts = lon_count // groups
    sources = lat_count * parts
    part_rows = tile_rows // parts
    chunk_rows = part_rows // CHUNKS
    total_rows = tile_rows * lat_count
    total_cols = tile_cols * lon_count
    kept_rows = total_rows // 2
    modes = total_cols // 4 // sources
    slots = modes_in.shape[1] // part_rows
    span = chunk_rows * slots
    factor = 1.0 / math.sqrt(total_rows * total_cols)
    lat = lax.axis_index("lat")
    lon = lax.axis_index("lon")
    my_group = lon // parts
    my_part = lax.rem(lon, parts)
    my_source = lat * parts + my_part

    def lon_device(index):
        return (lat, index)

    def mode_device(index):
        return (index // parts, my_group * parts + lax.rem(index, parts))

    barrier = pltpu.get_barrier_semaphore()

    @pl.loop(1, lon_count)
    def _(step):
        pl.semaphore_signal(
            barrier,
            inc=1,
            device_id=lon_device(lax.rem(lon + step, lon_count)),
            device_id_type=MESH,
        )

    @pl.loop(1, sources)
    def _(step):
        pl.semaphore_signal(
            barrier,
            inc=1,
            device_id=mode_device(lax.rem(my_source + step, sources)),
            device_id_type=MESH,
        )

    pl.semaphore_wait(barrier, lon_count + sources - 2)

    def lon_piece(chunk, owner):
        group = owner // parts
        part = lax.rem(owner, parts)
        return mixer_ref.at[
            pl.ds(part * part_rows + chunk * chunk_rows, chunk_rows),
            :,
            pl.ds(pl.multiple_of(group * LANES, LANES), LANES),
        ]

    def column_piece(ref, chunk, owner):
        return ref.at[
            pl.ds(chunk * chunk_rows, chunk_rows),
            pl.ds(pl.multiple_of(owner * tile_cols, 16), tile_cols),
            :,
        ]

    def mode_piece(ref, chunk, owner):
        return ref.at[owner, pl.ds(chunk * span, span), :]

    def tile_piece(chunk, owner):
        group = owner // parts
        part = lax.rem(owner, parts)
        return out_ref.at[
            pl.ds(part * part_rows + chunk * chunk_rows, chunk_rows),
            :,
            pl.ds(pl.multiple_of(group * LANES, LANES), LANES),
        ]

    def send_all(chunk, count, mine, device, source, target, send_sem, recv_sem):
        pltpu.make_async_copy(source(mine), target(mine), recv_sem.at[chunk, mine]).start()

        @pl.loop(1, count)
        def _(step):
            peer = lax.rem(mine + step, count)
            pltpu.make_async_remote_copy(
                src_ref=source(peer),
                dst_ref=target(mine),
                send_sem=send_sem.at[chunk, peer],
                recv_sem=recv_sem.at[chunk, mine],
                device_id=device(peer),
                device_id_type=MESH,
            ).start()

    def wait_all(chunk, count, mine, device, source, target, send_sem, recv_sem):
        pltpu.make_async_copy(source(mine), target(mine), recv_sem.at[chunk, mine]).wait()

        @pl.loop(1, count)
        def _(step):
            peer = lax.rem(mine + step, count)
            pltpu.make_async_remote_copy(
                src_ref=source(peer),
                dst_ref=target(peer),
                send_sem=send_sem.at[chunk, peer],
                recv_sem=recv_sem.at[chunk, peer],
                device_id=device(peer),
                device_id_type=MESH,
            ).wait_recv()

    def wait_sent(chunk, count, mine, device, source, target, send_sem, recv_sem):
        @pl.loop(1, count)
        def _(step):
            peer = lax.rem(mine + step, count)
            pltpu.make_async_remote_copy(
                src_ref=source(peer),
                dst_ref=target(peer),
                send_sem=send_sem.at[chunk, peer],
                recv_sem=recv_sem.at[chunk, peer],
                device_id=device(peer),
                device_id_type=MESH,
            ).wait_send()

    def lon_plan(chunk):
        return (
            chunk,
            lon_count,
            lon,
            lon_device,
            lambda owner: lon_piece(chunk, owner),
            lambda owner: column_piece(columns_in, chunk, owner),
            lon_send,
            lon_recv,
        )

    def mode_plan(chunk):
        return (
            chunk,
            sources,
            my_source,
            mode_device,
            lambda owner: mode_piece(modes_out, chunk, owner),
            lambda owner: mode_piece(modes_in, chunk, owner),
            mode_send,
            mode_recv,
        )

    def back_plan(chunk):
        return (
            chunk,
            sources,
            my_source,
            mode_device,
            lambda owner: mode_piece(back_out, chunk, owner),
            lambda owner: mode_piece(back_in, chunk, owner),
            back_send,
            back_recv,
        )

    def tile_plan(chunk):
        return (
            chunk,
            lon_count,
            lon,
            lon_device,
            lambda owner: column_piece(columns_out, chunk, owner),
            lambda owner: tile_piece(chunk, owner),
            tile_send,
            tile_recv,
        )

    for chunk in range(CHUNKS):
        send_all(*lon_plan(chunk))
    for chunk in range(CHUNKS):
        wait_all(*lon_plan(chunk))
        first = chunk * chunk_rows
        field = jnp.concatenate([columns_in[first + row] for row in range(chunk_rows)], axis=1)
        along = jnp.dot(forward_ref[...], field, preferred_element_type=jnp.float32)
        along = jnp.concatenate(
            [
                along[:, row * LANES : (row + 1) * LANES].reshape(sources, slots, LANES)
                for row in range(chunk_rows)
            ],
            axis=1,
        )
        modes_out[:, chunk * span : (chunk + 1) * span, :] = along.astype(jnp.bfloat16)
        send_all(*mode_plan(chunk))
    for chunk in range(CHUNKS):
        wait_all(*mode_plan(chunk))
    modes_work[...] = modes_in[...].astype(jnp.float32).reshape(modes_work.shape)

    batch = 4 if modes % 4 == 0 else modes
    for start in range(0, modes, batch):
        members = range(start, start + batch)

        def every_row(slot):
            return modes_work[pl.ds(slot, total_rows, stride=slots), :].astype(jnp.bfloat16)

        field = jnp.concatenate(
            [
                jnp.concatenate([every_row(2 * mode), every_row(2 * mode + 1)], axis=0)
                for mode in members
            ],
            axis=1,
        )
        spectrum = (
            jnp.dot(lat_forward_ref[...], field, preferred_element_type=jnp.float32) * factor
        )
        spectrum = jnp.concatenate(
            [
                jnp.concatenate(
                    [
                        spectrum[:kept_rows, index * LANES : (index + 1) * LANES],
                        spectrum[kept_rows:, index * LANES : (index + 1) * LANES],
                    ],
                    axis=1,
                )
                for index in range(batch)
            ],
            axis=0,
        ).astype(jnp.bfloat16)
        hidden = jnp.dot(spectrum, weight_one_ref[...], preferred_element_type=jnp.float32)
        hidden = jnp.maximum(hidden + bias_one_ref[...], 0.0).astype(jnp.bfloat16)
        filtered = jnp.dot(hidden, weight_two_ref[...], preferred_element_type=jnp.float32)
        filtered = filtered + bias_two_ref[...]
        filtered = jnp.concatenate(
            [
                jnp.concatenate(
                    [
                        filtered[index * kept_rows : (index + 1) * kept_rows, :LANES],
                        filtered[index * kept_rows : (index + 1) * kept_rows, LANES:],
                    ],
                    axis=0,
                )
                for index in range(batch)
            ],
            axis=1,
        ).astype(jnp.bfloat16)
        rows = jnp.dot(lat_inverse_ref[...], filtered, preferred_element_type=jnp.float32)
        for index, mode in enumerate(members):
            lanes = slice(index * LANES, (index + 1) * LANES)
            modes_work[pl.ds(2 * mode, total_rows, stride=slots), :] = rows[:total_rows, lanes]
            modes_work[pl.ds(2 * mode + 1, total_rows, stride=slots), :] = rows[total_rows:, lanes]
    back_out[...] = modes_work[...].reshape(back_out.shape).astype(jnp.bfloat16)
    for chunk in range(CHUNKS):
        send_all(*back_plan(chunk))
    for chunk in range(CHUNKS):
        wait_all(*back_plan(chunk))
        first = chunk * chunk_rows
        piece = back_in[:, chunk * span : (chunk + 1) * span, :].astype(jnp.float32)
        field = jnp.concatenate(
            [
                piece[:, row * slots : (row + 1) * slots, :].reshape(sources * slots, LANES)
                for row in range(chunk_rows)
            ],
            axis=1,
        ).astype(jnp.bfloat16)
        whole = jnp.dot(inverse_ref[...], field, preferred_element_type=jnp.float32) * factor
        for row in range(chunk_rows):
            columns_out[first + row] = whole[:, row * LANES : (row + 1) * LANES].astype(
                jnp.bfloat16
            )
        send_all(*tile_plan(chunk))
    for chunk in range(CHUNKS):
        wait_all(*tile_plan(chunk))
    for chunk in range(CHUNKS):
        for plan in (lon_plan, mode_plan, back_plan, tile_plan):
            wait_sent(*plan(chunk))


def paired_weights(weight, bias, group):
    blocks = LANES // weight.shape[2]
    part = lax.dynamic_slice_in_dim(weight, group * blocks, blocks, axis=1)
    eye = jnp.eye(blocks, dtype=weight.dtype)
    wide = (part[:, :, :, None, :] * eye[None, :, None, :, None]).reshape(2, LANES, LANES)
    joined = jnp.concatenate(
        [
            jnp.concatenate([wide[0], wide[1]], axis=1),
            jnp.concatenate([-wide[1], wide[0]], axis=1),
        ],
        axis=0,
    ).astype(jnp.bfloat16)
    offset = lax.dynamic_slice_in_dim(bias, group * blocks, blocks, axis=1).reshape(1, 2 * LANES)
    return joined, offset


def spectral_mixer(mixer_in, first_weight, first_bias, second_weight, second_bias):
    tile_rows, tile_cols, features = mixer_in.shape
    lat_count = lax.axis_size("lat")
    lon_count = lax.axis_size("lon")
    groups = features // LANES
    parts = lon_count // groups
    sources = lat_count * parts
    part_rows = tile_rows // parts
    total_rows = tile_rows * lat_count
    total_cols = tile_cols * lon_count
    modes = total_cols // 4 // sources
    slots = -(-2 * modes // 8) * 8
    tables = mixer_tables(total_rows, total_cols, sources, slots)
    group = lax.axis_index("lon") // parts
    weight_one, bias_one = paired_weights(first_weight, first_bias, group)
    weight_two, bias_two = paired_weights(second_weight, second_bias, group)
    vmem = pl.BlockSpec(memory_space=pltpu.VMEM)
    modes_shape = (sources, part_rows * slots, LANES)
    return pl.pallas_call(
        functools.partial(mixer_kernel, lat_count, lon_count),
        out_shape=jax.ShapeDtypeStruct(mixer_in.shape, jnp.bfloat16),
        in_specs=[vmem] * 9,
        out_specs=vmem,
        scratch_shapes=[
            pltpu.VMEM((part_rows, total_cols, LANES), jnp.bfloat16),
            pltpu.VMEM(modes_shape, jnp.bfloat16),
            pltpu.VMEM(modes_shape, jnp.bfloat16),
            pltpu.VMEM((sources * part_rows * slots, LANES), jnp.float32),
            pltpu.VMEM(modes_shape, jnp.bfloat16),
            pltpu.VMEM(modes_shape, jnp.bfloat16),
            pltpu.VMEM((part_rows, total_cols, LANES), jnp.bfloat16),
        ]
        + [
            pltpu.SemaphoreType.DMA((CHUNKS, count))
            for count in (lon_count, sources, sources, lon_count)
            for _ in range(2)
        ],
        compiler_params=pltpu.CompilerParams(
            collective_id=1, has_side_effects=True, vmem_limit_bytes=48 * 1024 * 1024
        ),
        name="spectral_mixer",
    )(mixer_in, *tables, weight_one, bias_one, weight_two, bias_two)


def shards(
    grid_tokens,
    attention_gain,
    score_weight,
    value_weight,
    output_weight,
    mixer_gain,
    first_weight,
    first_bias,
    second_weight,
    second_bias,
):
    tile_rows, tile_cols, features = grid_tokens.shape
    lat_count = lax.axis_size("lat")
    lon_count = lax.axis_size("lon")
    total_rows = tile_rows * lat_count
    total_cols = tile_cols * lon_count
    head_size = features // HEADS
    span = 2 * RADIUS + 1
    normed_in = normed(grid_tokens, attention_gain)
    flat_in = normed_in.reshape(tile_rows * tile_cols, features)
    queries = jnp.dot(
        flat_in, score_weight[:, :features], preferred_element_type=jnp.float32
    ).astype(jnp.bfloat16)
    queries = queries.reshape(tile_rows, tile_cols, features)
    kv_weight = jnp.concatenate([score_weight[:, features:], value_weight], axis=1)
    projected = jnp.dot(flat_in, kv_weight, preferred_element_type=jnp.float32).astype(jnp.bfloat16)
    projected = projected.reshape(tile_rows, tile_cols, 2 * features)
    padded = padded_2(projected, (("lat", 0), ("lon", 1)), RADIUS)
    key_pad = padded[:, :, :features]
    value_pad = padded[:, :, features:]
    block_rows = 12
    pad_cols = tile_cols + 2 * RADIUS
    row_anchor = lax.axis_index("lat") * tile_rows
    column_gap = (
        jnp.arange(pad_cols, dtype=jnp.int32)[None, :]
        - jnp.arange(tile_cols, dtype=jnp.int32)[:, None]
    )
    column_inside = (column_gap >= 0) & (column_gap < span)
    factor = 1.0 / math.sqrt(head_size)
    pieces = []
    for row_start in range(0, tile_rows, block_rows):
        query_rows = row_anchor + row_start + jnp.arange(block_rows, dtype=jnp.int32)
        window_start = jnp.clip(query_rows - RADIUS, 0, total_rows - span)
        key_rows = (
            row_anchor + row_start - RADIUS + jnp.arange(block_rows + 2 * RADIUS, dtype=jnp.int32)
        )
        row_inside = (key_rows[None, :] >= window_start[:, None]) & (
            key_rows[None, :] < window_start[:, None] + span
        )
        allowed = (row_inside[:, None, :, None] & column_inside[None, :, None, :]).reshape(
            block_rows * tile_cols, -1
        )
        query_block = queries[row_start : row_start + block_rows].reshape(-1, features)
        key_block = key_pad[row_start : row_start + block_rows + 2 * RADIUS].reshape(-1, features)
        value_block = value_pad[row_start : row_start + block_rows + 2 * RADIUS].reshape(
            -1, features
        )
        head_outputs = []
        for head_index in range(HEADS):
            lower = head_index * head_size
            upper = lower + head_size
            scores = (
                jnp.einsum(
                    "qd,kd->qk",
                    query_block[:, lower:upper],
                    key_block[:, lower:upper],
                    preferred_element_type=jnp.float32,
                )
                * factor
            )
            scores = jnp.where(allowed, scores, -1e30)
            largest = jnp.max(scores, axis=1, keepdims=True)
            weights = jnp.exp(scores - largest)
            probs = (weights / jnp.sum(weights, axis=1, keepdims=True)).astype(jnp.bfloat16)
            head_outputs.append(
                jnp.dot(
                    probs, value_block[:, lower:upper], preferred_element_type=jnp.float32
                ).astype(jnp.bfloat16)
            )
        pieces.append(jnp.concatenate(head_outputs, axis=1))
    attended = jnp.concatenate(pieces, axis=0)
    projected_out = jnp.dot(attended, output_weight, preferred_element_type=jnp.float32)
    after_attention = (
        grid_tokens.astype(jnp.float32).reshape(-1, features) + projected_out
    ).astype(jnp.bfloat16)
    after_attention = after_attention.reshape(tile_rows, tile_cols, features)
    mixer_in = normed(after_attention, mixer_gain)
    tile_back = spectral_mixer(mixer_in, first_weight, first_bias, second_weight, second_bias)
    summed = (
        after_attention.astype(jnp.float32)
        + mixer_in.astype(jnp.float32)
        + tile_back.astype(jnp.float32)
    )
    return summed.astype(jnp.bfloat16)


def solution(mesh):
    placed = (P("lat", "lon", None), P(), P(), P(), P(), P(), P(), P(), P(), P())
    return jax.shard_map(
        shards, mesh=mesh, in_specs=placed, out_specs=P("lat", "lon", None), check_vma=False
    )
```

```python
import functools
import math

import jax
import jax.numpy as jnp
import numpy as np
from jax import lax
from jax.experimental import pallas as pl
from jax.experimental.pallas import tpu as pltpu
from jax.sharding import PartitionSpec as P

HEADS = 8
RADIUS = 6


LANES = 128
CHUNKS = 3
MESH = pl.DeviceIdType.MESH


def mixer_tables(total_rows, total_cols, sources, slots):
    kept_rows = total_rows // 2
    kept_cols = total_cols // 4
    modes = kept_cols // sources
    column = np.arange(total_cols)
    angle = 2.0 * np.pi * (np.outer(np.arange(kept_cols), column) % total_cols) / total_cols
    cosine = np.cos(angle).reshape(sources, modes, total_cols)
    sine = np.sin(angle).reshape(sources, modes, total_cols)
    forward = np.zeros((sources, slots, total_cols))
    forward[:, 0 : 2 * modes : 2] = cosine
    forward[:, 1 : 2 * modes : 2] = -sine
    doubled = np.full((kept_cols, 1), 2.0)
    doubled[0] = 1.0
    inverse = (forward.reshape(sources, slots, total_cols)).copy()
    inverse[:, 0 : 2 * modes : 2] *= doubled.reshape(sources, modes, 1)
    inverse[:, 1 : 2 * modes : 2] *= doubled.reshape(sources, modes, 1)
    forward = forward.reshape(sources * slots, total_cols)
    inverse = inverse.reshape(sources * slots, total_cols).T
    frequency = np.arange(kept_rows)
    frequency = frequency + np.where(frequency >= kept_rows // 2, total_rows - kept_rows, 0)
    angle = 2.0 * np.pi * (np.outer(frequency, np.arange(total_rows)) % total_rows) / total_rows
    cosine = np.cos(angle)
    sine = np.sin(angle)
    lat_forward = np.block([[cosine, sine], [-sine, cosine]])
    lat_inverse = np.block([[cosine.T, -sine.T], [sine.T, cosine.T]])
    return tuple(
        np.asarray(table, dtype=jnp.bfloat16)
        for table in (forward, lat_forward, lat_inverse, inverse)
    )


def mixer_kernel(
    lat_count,
    lon_count,
    mixer_ref,
    forward_ref,
    lat_forward_ref,
    lat_inverse_ref,
    inverse_ref,
    weight_one_ref,
    bias_one_ref,
    weight_two_ref,
    bias_two_ref,
    out_ref,
    columns_in,
    modes_out,
    modes_in,
    modes_work,
    back_out,
    back_in,
    columns_out,
    lon_send,
    lon_recv,
    mode_send,
    mode_recv,
    back_send,
    back_recv,
    tile_send,
    tile_recv,
):
    tile_rows, tile_cols, features = mixer_ref.shape
    groups = features // LANES
    parts = lon_count // groups
    sources = lat_count * parts
    part_rows = tile_rows // parts
    chunk_rows = part_rows // CHUNKS
    total_rows = tile_rows * lat_count
    total_cols = tile_cols * lon_count
    kept_rows = total_rows // 2
    modes = total_cols // 4 // sources
    slots = modes_in.shape[1] // part_rows
    span = chunk_rows * slots
    factor = 1.0 / math.sqrt(total_rows * total_cols)
    lat = lax.axis_index("lat")
    lon = lax.axis_index("lon")
    my_group = lon // parts
    my_part = lax.rem(lon, parts)
    my_source = lat * parts + my_part

    def lon_device(index):
        return (lat, index)

    def mode_device(index):
        return (index // parts, my_group * parts + lax.rem(index, parts))

    barrier = pltpu.get_barrier_semaphore()

    @pl.loop(1, lon_count)
    def _(step):
        pl.semaphore_signal(
            barrier,
            inc=1,
            device_id=lon_device(lax.rem(lon + step, lon_count)),
            device_id_type=MESH,
        )

    @pl.loop(1, sources)
    def _(step):
        pl.semaphore_signal(
            barrier,
            inc=1,
            device_id=mode_device(lax.rem(my_source + step, sources)),
            device_id_type=MESH,
        )

    pl.semaphore_wait(barrier, lon_count + sources - 2)

    def lon_piece(chunk, owner):
        group = owner // parts
        part = lax.rem(owner, parts)
        return mixer_ref.at[
            pl.ds(part * part_rows + chunk * chunk_rows, chunk_rows),
            :,
            pl.ds(pl.multiple_of(group * LANES, LANES), LANES),
        ]

    def column_piece(ref, chunk, owner):
        return ref.at[
            pl.ds(chunk * chunk_rows, chunk_rows),
            pl.ds(pl.multiple_of(owner * tile_cols, 16), tile_cols),
            :,
        ]

    def mode_piece(ref, chunk, owner):
        return ref.at[owner, pl.ds(chunk * span, span), :]

    def tile_piece(chunk, owner):
        group = owner // parts
        part = lax.rem(owner, parts)
        return out_ref.at[
            pl.ds(part * part_rows + chunk * chunk_rows, chunk_rows),
            :,
            pl.ds(pl.multiple_of(group * LANES, LANES), LANES),
        ]

    def send_all(chunk, count, mine, device, source, target, send_sem, recv_sem):
        pltpu.make_async_copy(source(mine), target(mine), recv_sem.at[chunk, mine]).start()

        @pl.loop(1, count)
        def _(step):
            peer = lax.rem(mine + step, count)
            pltpu.make_async_remote_copy(
                src_ref=source(peer),
                dst_ref=target(mine),
                send_sem=send_sem.at[chunk, peer],
                recv_sem=recv_sem.at[chunk, mine],
                device_id=device(peer),
                device_id_type=MESH,
            ).start()

    def wait_all(chunk, count, mine, device, source, target, send_sem, recv_sem):
        pltpu.make_async_copy(source(mine), target(mine), recv_sem.at[chunk, mine]).wait()

        @pl.loop(1, count)
        def _(step):
            peer = lax.rem(mine + step, count)
            pltpu.make_async_remote_copy(
                src_ref=source(peer),
                dst_ref=target(peer),
                send_sem=send_sem.at[chunk, peer],
                recv_sem=recv_sem.at[chunk, peer],
                device_id=device(peer),
                device_id_type=MESH,
            ).wait_recv()

    def wait_sent(chunk, count, mine, device, source, target, send_sem, recv_sem):
        @pl.loop(1, count)
        def _(step):
            peer = lax.rem(mine + step, count)
            pltpu.make_async_remote_copy(
                src_ref=source(peer),
                dst_ref=target(peer),
                send_sem=send_sem.at[chunk, peer],
                recv_sem=recv_sem.at[chunk, peer],
                device_id=device(peer),
                device_id_type=MESH,
            ).wait_send()

    def lon_plan(chunk):
        return (
            chunk,
            lon_count,
            lon,
            lon_device,
            lambda owner: lon_piece(chunk, owner),
            lambda owner: column_piece(columns_in, chunk, owner),
            lon_send,
            lon_recv,
        )

    def mode_plan(chunk):
        return (
            chunk,
            sources,
            my_source,
            mode_device,
            lambda owner: mode_piece(modes_out, chunk, owner),
            lambda owner: mode_piece(modes_in, chunk, owner),
            mode_send,
            mode_recv,
        )

    def back_plan(chunk):
        return (
            chunk,
            sources,
            my_source,
            mode_device,
            lambda owner: mode_piece(back_out, chunk, owner),
            lambda owner: mode_piece(back_in, chunk, owner),
            back_send,
            back_recv,
        )

    def tile_plan(chunk):
        return (
            chunk,
            lon_count,
            lon,
            lon_device,
            lambda owner: column_piece(columns_out, chunk, owner),
            lambda owner: tile_piece(chunk, owner),
            tile_send,
            tile_recv,
        )

    for chunk in range(CHUNKS):
        send_all(*lon_plan(chunk))
    for chunk in range(CHUNKS):
        wait_all(*lon_plan(chunk))
        first = chunk * chunk_rows
        field = jnp.concatenate([columns_in[first + row] for row in range(chunk_rows)], axis=1)
        along = jnp.dot(forward_ref[...], field, preferred_element_type=jnp.float32)
        along = jnp.concatenate(
            [
                along[:, row * LANES : (row + 1) * LANES].reshape(sources, slots, LANES)
                for row in range(chunk_rows)
            ],
            axis=1,
        )
        modes_out[:, chunk * span : (chunk + 1) * span, :] = along.astype(jnp.bfloat16)
        send_all(*mode_plan(chunk))
    for chunk in range(CHUNKS):
        wait_all(*mode_plan(chunk))
    modes_work[...] = modes_in[...].astype(jnp.float32).reshape(modes_work.shape)

    batch = 4 if modes % 4 == 0 else modes
    for start in range(0, modes, batch):
        members = range(start, start + batch)

        def every_row(slot):
            return modes_work[pl.ds(slot, total_rows, stride=slots), :].astype(jnp.bfloat16)

        field = jnp.concatenate(
            [
                jnp.concatenate([every_row(2 * mode), every_row(2 * mode + 1)], axis=0)
                for mode in members
            ],
            axis=1,
        )
        spectrum = (
            jnp.dot(lat_forward_ref[...], field, preferred_element_type=jnp.float32) * factor
        )
        spectrum = jnp.concatenate(
            [
                jnp.concatenate(
                    [
                        spectrum[:kept_rows, index * LANES : (index + 1) * LANES],
                        spectrum[kept_rows:, index * LANES : (index + 1) * LANES],
                    ],
                    axis=1,
                )
                for index in range(batch)
            ],
            axis=0,
        ).astype(jnp.bfloat16)
        hidden = jnp.dot(spectrum, weight_one_ref[...], preferred_element_type=jnp.float32)
        hidden = jnp.maximum(hidden + bias_one_ref[...], 0.0).astype(jnp.bfloat16)
        filtered = jnp.dot(hidden, weight_two_ref[...], preferred_element_type=jnp.float32)
        filtered = filtered + bias_two_ref[...]
        filtered = jnp.concatenate(
            [
                jnp.concatenate(
                    [
                        filtered[index * kept_rows : (index + 1) * kept_rows, :LANES],
                        filtered[index * kept_rows : (index + 1) * kept_rows, LANES:],
                    ],
                    axis=0,
                )
                for index in range(batch)
            ],
            axis=1,
        ).astype(jnp.bfloat16)
        rows = jnp.dot(lat_inverse_ref[...], filtered, preferred_element_type=jnp.float32)
        for index, mode in enumerate(members):
            lanes = slice(index * LANES, (index + 1) * LANES)
            modes_work[pl.ds(2 * mode, total_rows, stride=slots), :] = rows[:total_rows, lanes]
            modes_work[pl.ds(2 * mode + 1, total_rows, stride=slots), :] = rows[total_rows:, lanes]
    back_out[...] = modes_work[...].reshape(back_out.shape).astype(jnp.bfloat16)
    for chunk in range(CHUNKS):
        send_all(*back_plan(chunk))
    for chunk in range(CHUNKS):
        wait_all(*back_plan(chunk))
        first = chunk * chunk_rows
        piece = back_in[:, chunk * span : (chunk + 1) * span, :].astype(jnp.float32)
        field = jnp.concatenate(
            [
                piece[:, row * slots : (row + 1) * slots, :].reshape(sources * slots, LANES)
                for row in range(chunk_rows)
            ],
            axis=1,
        ).astype(jnp.bfloat16)
        whole = jnp.dot(inverse_ref[...], field, preferred_element_type=jnp.float32) * factor
        for row in range(chunk_rows):
            columns_out[first + row] = whole[:, row * LANES : (row + 1) * LANES].astype(
                jnp.bfloat16
            )
        send_all(*tile_plan(chunk))
    for chunk in range(CHUNKS):
        wait_all(*tile_plan(chunk))
    for chunk in range(CHUNKS):
        for plan in (lon_plan, mode_plan, back_plan, tile_plan):
            wait_sent(*plan(chunk))


def paired_weights(weight, bias, group):
    blocks = LANES // weight.shape[2]
    part = lax.dynamic_slice_in_dim(weight, group * blocks, blocks, axis=1)
    eye = jnp.eye(blocks, dtype=weight.dtype)
    wide = (part[:, :, :, None, :] * eye[None, :, None, :, None]).reshape(2, LANES, LANES)
    joined = jnp.concatenate(
        [
            jnp.concatenate([wide[0], wide[1]], axis=1),
            jnp.concatenate([-wide[1], wide[0]], axis=1),
        ],
        axis=0,
    ).astype(jnp.bfloat16)
    offset = lax.dynamic_slice_in_dim(bias, group * blocks, blocks, axis=1).reshape(1, 2 * LANES)
    return joined, offset


def spectral_mixer(mixer_in, first_weight, first_bias, second_weight, second_bias):
    tile_rows, tile_cols, features = mixer_in.shape
    lat_count = lax.axis_size("lat")
    lon_count = lax.axis_size("lon")
    groups = features // LANES
    parts = lon_count // groups
    sources = lat_count * parts
    part_rows = tile_rows // parts
    total_rows = tile_rows * lat_count
    total_cols = tile_cols * lon_count
    modes = total_cols // 4 // sources
    slots = -(-2 * modes // 8) * 8
    tables = mixer_tables(total_rows, total_cols, sources, slots)
    group = lax.axis_index("lon") // parts
    weight_one, bias_one = paired_weights(first_weight, first_bias, group)
    weight_two, bias_two = paired_weights(second_weight, second_bias, group)
    vmem = pl.BlockSpec(memory_space=pltpu.VMEM)
    modes_shape = (sources, part_rows * slots, LANES)
    return pl.pallas_call(
        functools.partial(mixer_kernel, lat_count, lon_count),
        out_shape=jax.ShapeDtypeStruct(mixer_in.shape, jnp.bfloat16),
        in_specs=[vmem] * 9,
        out_specs=vmem,
        scratch_shapes=[
            pltpu.VMEM((part_rows, total_cols, LANES), jnp.bfloat16),
            pltpu.VMEM(modes_shape, jnp.bfloat16),
            pltpu.VMEM(modes_shape, jnp.bfloat16),
            pltpu.VMEM((sources * part_rows * slots, LANES), jnp.float32),
            pltpu.VMEM(modes_shape, jnp.bfloat16),
            pltpu.VMEM(modes_shape, jnp.bfloat16),
            pltpu.VMEM((part_rows, total_cols, LANES), jnp.bfloat16),
        ]
        + [
            pltpu.SemaphoreType.DMA((CHUNKS, count))
            for count in (lon_count, sources, sources, lon_count)
            for _ in range(2)
        ],
        compiler_params=pltpu.CompilerParams(
            collective_id=1, has_side_effects=True, vmem_limit_bytes=48 * 1024 * 1024
        ),
        name="spectral_mixer",
    )(mixer_in, *tables, weight_one, bias_one, weight_two, bias_two)


BLOCK_ROWS = 8
BLOCK_COLS = 16
EDGE = 16


def attention_kernel(
    lat_count,
    lon_count,
    token_ref,
    gain_ref,
    score_ref,
    value_ref,
    output_ref,
    mixer_gain_ref,
    after_ref,
    mixer_ref,
    padded,
    query,
    key_value,
    bias,
    send_sem,
    recv_sem,
    own_sem,
):
    tile_rows, tile_cols, features = token_ref.shape
    total_rows = tile_rows * lat_count
    span = 2 * RADIUS + 1
    head_size = features // HEADS
    pairs = features // LANES
    lat = lax.axis_index("lat")
    lon = lax.axis_index("lon")
    has_upper = lat > 0
    has_lower = lat < lat_count - 1
    left = lax.rem(lon + lon_count - 1, lon_count)
    right = lax.rem(lon + 1, lon_count)

    send_rows = {-1: (0, RADIUS), 0: (0, tile_rows), 1: (tile_rows - RADIUS, RADIUS)}
    land_rows = {
        -1: (tile_rows + RADIUS, RADIUS),
        0: (RADIUS, tile_rows),
        1: (0, RADIUS),
    }
    send_cols = {-1: (0, EDGE), 0: (0, tile_cols), 1: (tile_cols - EDGE, EDGE)}
    land_cols = {-1: (tile_cols + EDGE, EDGE), 0: (EDGE, tile_cols), 1: (0, EDGE)}
    moves = [(0, -1), (0, 1)] + [(down, across) for down in (-1, 1) for across in (0, -1, 1)]

    def transfer(index):
        down, across = moves[index]
        target = {-1: left, 0: lon, 1: right}[across]
        return pltpu.make_async_remote_copy(
            src_ref=token_ref.at[pl.ds(*send_rows[down]), pl.ds(*send_cols[across]), :],
            dst_ref=padded.at[pl.ds(*land_rows[down]), pl.ds(*land_cols[across]), :],
            send_sem=send_sem.at[index],
            recv_sem=recv_sem.at[index],
            device_id=(lat + down, target),
            device_id_type=MESH,
        )

    barrier = pltpu.get_barrier_semaphore()

    def greet(row):
        for column in (left, lon, right):
            pl.semaphore_signal(
                barrier, inc=1, device_id=(row, column), device_id_type=MESH
            )

    for column in (left, right):
        pl.semaphore_signal(barrier, inc=1, device_id=(lat, column), device_id_type=MESH)

    @pl.when(has_upper)
    def _():
        greet(lat - 1)

    @pl.when(has_lower)
    def _():
        greet(lat + 1)

    above = (lat + lat_count - 1) // lat_count
    below = (2 * lat_count - 2 - lat) // lat_count
    pl.semaphore_wait(barrier, 2 + 3 * (above + below))

    for index in (0, 1):
        transfer(index).start()

    @pl.when(has_upper)
    def _():
        for index in (2, 3, 4):
            transfer(index).start()

    @pl.when(has_lower)
    def _():
        for index in (5, 6, 7):
            transfer(index).start()

    own = pltpu.make_async_copy(
        token_ref,
        padded.at[pl.ds(RADIUS, tile_rows), pl.ds(EDGE, tile_cols), :],
        own_sem,
    )
    own.start()
    blank = jnp.zeros((RADIUS, tile_cols + 2 * EDGE, features), jnp.bfloat16)

    @pl.when(jnp.logical_not(has_upper))
    def _():
        padded[:RADIUS] = blank

    @pl.when(jnp.logical_not(has_lower))
    def _():
        padded[tile_rows + RADIUS :] = blank

    def norm(data, gain):
        centre = jnp.mean(data, axis=-1, keepdims=True)
        centred = data - centre
        spread = jnp.mean(centred * centred, axis=-1, keepdims=True)
        return (centred * lax.rsqrt(spread + 1e-05) * gain).astype(jnp.bfloat16)

    def spread_pairs(ref, base, rows, values, cols):
        shaped = values.astype(jnp.bfloat16).reshape(RADIUS, cols, values.shape[1])
        for pair in range(values.shape[1] // LANES):
            ref[base + pair, rows] = shaped[:, :, pair * LANES : (pair + 1) * LANES]

    scale = 1.0 / math.sqrt(head_size)

    @pl.loop(0, tile_rows // RADIUS)
    def _(step):
        rows = pl.ds(step * RADIUS, RADIUS)
        data = token_ref[rows].astype(jnp.float32).reshape(-1, features)
        inputs = norm(data, gain_ref[...])
        values = jnp.dot(inputs, score_ref[:, :features], preferred_element_type=jnp.float32)
        values = values.astype(jnp.bfloat16).astype(jnp.float32) * scale
        spread_pairs(query, 0, rows, values, tile_cols)

    own.wait()
    for index in (0, 1):
        transfer(index).wait()

    @pl.when(has_lower)
    def _():
        for index in (2, 3, 4):
            transfer(index).wait_recv()

    @pl.when(has_upper)
    def _():
        for index in (5, 6, 7):
            transfer(index).wait_recv()

    near = EDGE // 2
    wide = tile_cols + 2 * near

    @pl.loop(0, tile_rows // RADIUS + 2)
    def _(step):
        rows = pl.ds(step * RADIUS, RADIUS)
        data = padded[rows].astype(jnp.float32)[:, near : near + wide, :].reshape(-1, features)
        inputs = norm(data, gain_ref[...])
        keys = jnp.dot(inputs, score_ref[:, features:], preferred_element_type=jnp.float32)
        spread_pairs(key_value, 0, rows, keys, wide)
        values = jnp.dot(inputs, value_ref[...], preferred_element_type=jnp.float32)
        spread_pairs(key_value, pairs, rows, values, wide)

    block = BLOCK_ROWS * BLOCK_COLS
    key_rows = BLOCK_ROWS + 2 * RADIUS
    key_cols = BLOCK_COLS + 2 * near
    reach = key_rows * key_cols
    col_blocks = tile_cols // BLOCK_COLS

    @pl.loop(0, (tile_rows // BLOCK_ROWS) * col_blocks)
    def _(step):
        row = step // col_blocks * BLOCK_ROWS
        col = pl.multiple_of(lax.rem(step, col_blocks) * BLOCK_COLS, BLOCK_COLS)
        token = lax.broadcasted_iota(jnp.int32, (block, reach), 0)
        other = lax.broadcasted_iota(jnp.int32, (block, reach), 1)
        top = lat * tile_rows + row
        start = jnp.clip(top + token // BLOCK_COLS - RADIUS, 0, total_rows - span)
        down = top - RADIUS + other // key_cols - start
        across = other % key_cols - near - token % BLOCK_COLS
        inside = (down >= 0) & (down < span) & (across >= -RADIUS) & (across <= RADIUS)
        bias[...] = jnp.where(inside, 0.0, -1e30)
        lower_lane = lax.broadcasted_iota(jnp.int32, (block, LANES), 1) < head_size
        heads = []
        for pair in range(pairs):
            asked = query[pair, pl.ds(row, BLOCK_ROWS), pl.ds(col, BLOCK_COLS), :]
            asked = asked.reshape(block, LANES).astype(jnp.float32)
            asked = jnp.concatenate(
                [jnp.where(lower_lane, asked, 0.0), jnp.where(lower_lane, 0.0, asked)], axis=0
            ).astype(jnp.bfloat16)
            window = (pl.ds(row, key_rows), pl.ds(col, key_cols), slice(None))
            keys = key_value[(pair, *window)].reshape(reach, LANES)
            values = key_value[(pairs + pair, *window)].reshape(reach, LANES)
            scores = lax.dot_general(
                asked, keys, (((1,), (1,)), ((), ())), preferred_element_type=jnp.float32
            )
            scores = (scores.reshape(2, block, reach) + bias[...]).reshape(2 * block, reach)
            weights = jnp.exp(scores - jnp.max(scores, axis=1, keepdims=True))
            total = jnp.sum(weights, axis=1, keepdims=True)
            mixed = jnp.dot(
                weights.astype(jnp.bfloat16), values, preferred_element_type=jnp.float32
            )
            mixed = mixed / total
            heads.append(jnp.where(lower_lane, mixed[:block], mixed[block:]))
        attended = jnp.concatenate(heads, axis=1).astype(jnp.bfloat16)
        place = (pl.ds(row, BLOCK_ROWS), pl.ds(col, BLOCK_COLS), slice(None))
        after = token_ref[place].astype(jnp.float32).reshape(block, features)
        after = after + jnp.dot(attended, output_ref[...], preferred_element_type=jnp.float32)
        after = after.astype(jnp.bfloat16)
        shape = (BLOCK_ROWS, BLOCK_COLS, features)
        after_ref[place] = after.reshape(shape)
        mixer_ref[place] = norm(after.astype(jnp.float32), mixer_gain_ref[...]).reshape(shape)

    @pl.when(has_upper)
    def _():
        for index in (2, 3, 4):
            transfer(index).wait_send()

    @pl.when(has_lower)
    def _():
        for index in (5, 6, 7):
            transfer(index).wait_send()


def attention(tokens, gain, score_weight, value_weight, output_weight, mixer_gain):
    tile_rows, tile_cols, features = tokens.shape
    pairs = features // LANES
    padded_rows = tile_rows + 2 * RADIUS
    vmem = pl.BlockSpec(memory_space=pltpu.VMEM)
    block = BLOCK_ROWS * BLOCK_COLS
    reach = (BLOCK_ROWS + 2 * RADIUS) * (BLOCK_COLS + EDGE)
    shape = jax.ShapeDtypeStruct(tokens.shape, jnp.bfloat16)
    return pl.pallas_call(
        functools.partial(attention_kernel, lax.axis_size("lat"), lax.axis_size("lon")),
        out_shape=(shape, shape),
        in_specs=[vmem] * 6,
        out_specs=(vmem, vmem),
        scratch_shapes=[
            pltpu.VMEM((padded_rows, tile_cols + 2 * EDGE, features), jnp.bfloat16),
            pltpu.VMEM((pairs, tile_rows, tile_cols, LANES), jnp.bfloat16),
            pltpu.VMEM((2 * pairs, padded_rows, tile_cols + EDGE, LANES), jnp.bfloat16),
            pltpu.VMEM((block, reach), jnp.float32),
            pltpu.SemaphoreType.DMA((8,)),
            pltpu.SemaphoreType.DMA((8,)),
            pltpu.SemaphoreType.DMA,
        ],
        compiler_params=pltpu.CompilerParams(
            collective_id=2, has_side_effects=True, vmem_limit_bytes=48 * 1024 * 1024
        ),
        name="attention",
    )(
        tokens,
        gain.reshape(1, features),
        score_weight,
        value_weight,
        output_weight,
        mixer_gain.reshape(1, features),
    )


def shards(
    grid_tokens,
    attention_gain,
    score_weight,
    value_weight,
    output_weight,
    mixer_gain,
    first_weight,
    first_bias,
    second_weight,
    second_bias,
):
    after_attention, mixer_in = attention(
        grid_tokens, attention_gain, score_weight, value_weight, output_weight, mixer_gain
    )
    spectral = spectral_mixer(mixer_in, first_weight, first_bias, second_weight, second_bias)
    summed = (
        after_attention.astype(jnp.float32)
        + mixer_in.astype(jnp.float32)
        + spectral.astype(jnp.float32)
    )
    return summed.astype(jnp.bfloat16)


def solution(mesh):
    placed = (P("lat", "lon", None), P(), P(), P(), P(), P(), P(), P(), P(), P())
    return jax.shard_map(
        shards, mesh=mesh, in_specs=placed, out_specs=P("lat", "lon", None), check_vma=False
    )
```

```python
import functools
import math

import jax
import jax.numpy as jnp
import numpy as np
from jax import lax
from jax.experimental import pallas as pl
from jax.experimental.pallas import tpu as pltpu
from jax.sharding import PartitionSpec as P

HEADS = 8
RADIUS = 6


LANES = 128
CHUNKS = 3
MESH = pl.DeviceIdType.MESH
BLOCK_ROWS = 8
BLOCK_COLS = 16
EDGE = 16


def mixer_tables(total_rows, total_cols, sources, slots):
    kept_rows = total_rows // 2
    kept_cols = total_cols // 4
    modes = kept_cols // sources
    column = np.arange(total_cols)
    angle = 2.0 * np.pi * (np.outer(np.arange(kept_cols), column) % total_cols) / total_cols
    cosine = np.cos(angle).reshape(sources, modes, total_cols)
    sine = np.sin(angle).reshape(sources, modes, total_cols)
    forward = np.zeros((sources, slots, total_cols))
    forward[:, 0 : 2 * modes : 2] = cosine
    forward[:, 1 : 2 * modes : 2] = -sine
    doubled = np.full((kept_cols, 1), 2.0)
    doubled[0] = 1.0
    inverse = (forward.reshape(sources, slots, total_cols)).copy()
    inverse[:, 0 : 2 * modes : 2] *= doubled.reshape(sources, modes, 1)
    inverse[:, 1 : 2 * modes : 2] *= doubled.reshape(sources, modes, 1)
    forward = forward.reshape(sources * slots, total_cols)
    inverse = inverse.reshape(sources * slots, total_cols).T
    frequency = np.arange(kept_rows)
    frequency = frequency + np.where(frequency >= kept_rows // 2, total_rows - kept_rows, 0)
    angle = 2.0 * np.pi * (np.outer(frequency, np.arange(total_rows)) % total_rows) / total_rows
    cosine = np.cos(angle)
    sine = np.sin(angle)
    lat_forward = np.block([[cosine, sine], [-sine, cosine]])
    lat_inverse = np.block([[cosine.T, -sine.T], [sine.T, cosine.T]])
    return tuple(
        np.asarray(table, dtype=jnp.bfloat16)
        for table in (forward, lat_forward, lat_inverse, inverse)
    )


def paired_weights(weight_ref, bias_ref, group, joined, offset):
    size = weight_ref.shape[2]
    blocks = LANES // size
    for index in range(blocks):
        source = group * blocks + index

        def wide(values):
            blank = jnp.zeros_like(values)
            return [values if place == index else blank for place in range(blocks)]

        real = weight_ref[0, source]
        imag = weight_ref[1, source]
        lower = index * size
        joined[lower : lower + size, :] = jnp.concatenate(
            wide(real) + wide(imag), axis=1
        ).astype(jnp.bfloat16)
        lower = LANES + index * size
        joined[lower : lower + size, :] = jnp.concatenate(
            wide(-imag) + wide(real), axis=1
        ).astype(jnp.bfloat16)
    offset[...] = jnp.concatenate(
        [
            bias_ref[part, pl.ds(group * blocks + index, 1), :]
            for part in range(2)
            for index in range(blocks)
        ],
        axis=1,
    )


def block_kernel(
    lat_count,
    lon_count,
    token_ref,
    gain_ref,
    score_ref,
    value_ref,
    output_ref,
    mixer_gain_ref,
    forward_ref,
    lat_forward_ref,
    lat_inverse_ref,
    inverse_ref,
    first_weight_ref,
    first_bias_ref,
    second_weight_ref,
    second_bias_ref,
    after_ref,
    mixer_ref,
    spectral_ref,
    padded,
    query,
    key_value,
    bias,
    columns_in,
    modes_out,
    modes_in,
    modes_work,
    back_out,
    back_in,
    columns_out,
    weight_one,
    bias_one,
    weight_two,
    bias_two,
    send_sem,
    recv_sem,
    own_sem,
    lon_send,
    lon_recv,
    mode_send,
    mode_recv,
    back_send,
    back_recv,
    tile_send,
    tile_recv,
):
    tile_rows, tile_cols, features = token_ref.shape
    total_rows = tile_rows * lat_count
    span = 2 * RADIUS + 1
    head_size = features // HEADS
    pairs = features // LANES
    lat = lax.axis_index("lat")
    lon = lax.axis_index("lon")
    has_upper = lat > 0
    has_lower = lat < lat_count - 1
    left = lax.rem(lon + lon_count - 1, lon_count)
    right = lax.rem(lon + 1, lon_count)

    groups = features // LANES
    parts = lon_count // groups
    sources = lat_count * parts
    part_rows = tile_rows // parts
    chunk_rows = part_rows // CHUNKS
    total_cols = tile_cols * lon_count
    kept_rows = total_rows // 2
    modes = total_cols // 4 // sources
    slots = modes_in.shape[1] // part_rows
    stretch = chunk_rows * slots
    factor = 1.0 / math.sqrt(total_rows * total_cols)
    my_group = lon // parts
    my_part = lax.rem(lon, parts)
    my_source = lat * parts + my_part

    def lon_device(index):
        return (lat, index)

    def mode_device(index):
        return (index // parts, my_group * parts + lax.rem(index, parts))

    send_rows = {-1: (0, RADIUS), 0: (0, tile_rows), 1: (tile_rows - RADIUS, RADIUS)}
    land_rows = {
        -1: (tile_rows + RADIUS, RADIUS),
        0: (RADIUS, tile_rows),
        1: (0, RADIUS),
    }
    send_cols = {-1: (0, EDGE), 0: (0, tile_cols), 1: (tile_cols - EDGE, EDGE)}
    land_cols = {-1: (tile_cols + EDGE, EDGE), 0: (EDGE, tile_cols), 1: (0, EDGE)}
    moves = [(0, -1), (0, 1)] + [(down, across) for down in (-1, 1) for across in (0, -1, 1)]

    def transfer(index):
        down, across = moves[index]
        target = {-1: left, 0: lon, 1: right}[across]
        return pltpu.make_async_remote_copy(
            src_ref=token_ref.at[pl.ds(*send_rows[down]), pl.ds(*send_cols[across]), :],
            dst_ref=padded.at[pl.ds(*land_rows[down]), pl.ds(*land_cols[across]), :],
            send_sem=send_sem.at[index],
            recv_sem=recv_sem.at[index],
            device_id=(lat + down, target),
            device_id_type=MESH,
        )

    barrier = pltpu.get_barrier_semaphore()

    def greet(row):
        for column in (left, lon, right):
            pl.semaphore_signal(
                barrier, inc=1, device_id=(row, column), device_id_type=MESH
            )

    for column in (left, right):
        pl.semaphore_signal(barrier, inc=1, device_id=(lat, column), device_id_type=MESH)

    @pl.loop(1, lon_count)
    def _(step):
        pl.semaphore_signal(
            barrier,
            inc=1,
            device_id=lon_device(lax.rem(lon + step, lon_count)),
            device_id_type=MESH,
        )

    @pl.loop(1, sources)
    def _(step):
        pl.semaphore_signal(
            barrier,
            inc=1,
            device_id=mode_device(lax.rem(my_source + step, sources)),
            device_id_type=MESH,
        )

    @pl.when(has_upper)
    def _():
        greet(lat - 1)

    @pl.when(has_lower)
    def _():
        greet(lat + 1)

    above = (lat + lat_count - 1) // lat_count
    below = (2 * lat_count - 2 - lat) // lat_count
    pl.semaphore_wait(barrier, lon_count + sources + 3 * (above + below))

    for index in (0, 1):
        transfer(index).start()

    @pl.when(has_upper)
    def _():
        for index in (2, 3, 4):
            transfer(index).start()

    @pl.when(has_lower)
    def _():
        for index in (5, 6, 7):
            transfer(index).start()

    own = pltpu.make_async_copy(
        token_ref,
        padded.at[pl.ds(RADIUS, tile_rows), pl.ds(EDGE, tile_cols), :],
        own_sem,
    )
    own.start()
    blank = jnp.zeros((RADIUS, tile_cols + 2 * EDGE, features), jnp.bfloat16)

    @pl.when(jnp.logical_not(has_upper))
    def _():
        padded[:RADIUS] = blank

    @pl.when(jnp.logical_not(has_lower))
    def _():
        padded[tile_rows + RADIUS :] = blank

    def norm(data, gain):
        centre = jnp.mean(data, axis=-1, keepdims=True)
        centred = data - centre
        spread = jnp.mean(centred * centred, axis=-1, keepdims=True)
        return (centred * lax.rsqrt(spread + 1e-05) * gain).astype(jnp.bfloat16)

    def spread_pairs(ref, base, rows, values, cols):
        shaped = values.astype(jnp.bfloat16).reshape(RADIUS, cols, values.shape[1])
        for pair in range(values.shape[1] // LANES):
            ref[base + pair, rows] = shaped[:, :, pair * LANES : (pair + 1) * LANES]

    scale = 1.0 / math.sqrt(head_size)

    @pl.loop(0, tile_rows // RADIUS)
    def _(step):
        rows = pl.ds(step * RADIUS, RADIUS)
        data = token_ref[rows].astype(jnp.float32).reshape(-1, features)
        inputs = norm(data, gain_ref[...])
        values = jnp.dot(inputs, score_ref[:, :features], preferred_element_type=jnp.float32)
        values = values.astype(jnp.bfloat16).astype(jnp.float32) * scale
        spread_pairs(query, 0, rows, values, tile_cols)

    paired_weights(first_weight_ref, first_bias_ref, my_group, weight_one, bias_one)
    paired_weights(second_weight_ref, second_bias_ref, my_group, weight_two, bias_two)
    own.wait()
    for index in (0, 1):
        transfer(index).wait()

    @pl.when(has_lower)
    def _():
        for index in (2, 3, 4):
            transfer(index).wait_recv()

    @pl.when(has_upper)
    def _():
        for index in (5, 6, 7):
            transfer(index).wait_recv()

    near = EDGE // 2
    wide = tile_cols + 2 * near

    @pl.loop(0, tile_rows // RADIUS + 2)
    def _(step):
        rows = pl.ds(step * RADIUS, RADIUS)
        data = padded[rows].astype(jnp.float32)[:, near : near + wide, :].reshape(-1, features)
        inputs = norm(data, gain_ref[...])
        keys = jnp.dot(inputs, score_ref[:, features:], preferred_element_type=jnp.float32)
        spread_pairs(key_value, 0, rows, keys, wide)
        values = jnp.dot(inputs, value_ref[...], preferred_element_type=jnp.float32)
        spread_pairs(key_value, pairs, rows, values, wide)

    block = BLOCK_ROWS * BLOCK_COLS
    key_rows = BLOCK_ROWS + 2 * RADIUS
    key_cols = BLOCK_COLS + 2 * near
    reach = key_rows * key_cols
    col_blocks = tile_cols // BLOCK_COLS

    def attend(row, col):
        lower_lane = lax.broadcasted_iota(jnp.int32, (block, LANES), 1) < head_size
        heads = []
        for pair in range(pairs):
            asked = query[pair, pl.ds(row, BLOCK_ROWS), pl.ds(col, BLOCK_COLS), :]
            asked = asked.reshape(block, LANES).astype(jnp.float32)
            asked = jnp.concatenate(
                [jnp.where(lower_lane, asked, 0.0), jnp.where(lower_lane, 0.0, asked)], axis=0
            ).astype(jnp.bfloat16)
            window = (pl.ds(row, key_rows), pl.ds(col, key_cols), slice(None))
            keys = key_value[(pair, *window)].reshape(reach, LANES)
            values = key_value[(pairs + pair, *window)].reshape(reach, LANES)
            scores = lax.dot_general(
                asked, keys, (((1,), (1,)), ((), ())), preferred_element_type=jnp.float32
            )
            scores = (scores.reshape(2, block, reach) + bias[...]).reshape(2 * block, reach)
            weights = jnp.exp(scores - jnp.max(scores, axis=1, keepdims=True))
            total = jnp.sum(weights, axis=1, keepdims=True)
            mixed = jnp.dot(
                weights.astype(jnp.bfloat16), values, preferred_element_type=jnp.float32
            )
            mixed = mixed / total
            heads.append(jnp.where(lower_lane, mixed[:block], mixed[block:]))
        attended = jnp.concatenate(heads, axis=1).astype(jnp.bfloat16)
        place = (pl.ds(row, BLOCK_ROWS), pl.ds(col, BLOCK_COLS), slice(None))
        after = token_ref[place].astype(jnp.float32).reshape(block, features)
        after = after + jnp.dot(attended, output_ref[...], preferred_element_type=jnp.float32)
        after = after.astype(jnp.bfloat16)
        shape = (BLOCK_ROWS, BLOCK_COLS, features)
        after_ref[place] = after.reshape(shape)
        mixer_ref[place] = norm(after.astype(jnp.float32), mixer_gain_ref[...]).reshape(shape)

    def lon_piece(chunk, owner):
        group = owner // parts
        part = lax.rem(owner, parts)
        return mixer_ref.at[
            pl.ds(part * part_rows + chunk * chunk_rows, chunk_rows),
            :,
            pl.ds(pl.multiple_of(group * LANES, LANES), LANES),
        ]

    def column_piece(ref, chunk, owner):
        return ref.at[
            pl.ds(chunk * chunk_rows, chunk_rows),
            pl.ds(pl.multiple_of(owner * tile_cols, 16), tile_cols),
            :,
        ]

    def mode_piece(ref, chunk, owner):
        return ref.at[owner, pl.ds(chunk * stretch, stretch), :]

    def tile_piece(chunk, owner):
        group = owner // parts
        part = lax.rem(owner, parts)
        return spectral_ref.at[
            pl.ds(part * part_rows + chunk * chunk_rows, chunk_rows),
            :,
            pl.ds(pl.multiple_of(group * LANES, LANES), LANES),
        ]

    def send_all(chunk, count, mine, device, source, target, send_sem, recv_sem):
        pltpu.make_async_copy(source(mine), target(mine), recv_sem.at[chunk, mine]).start()

        @pl.loop(1, count)
        def _(step):
            peer = lax.rem(mine + step, count)
            pltpu.make_async_remote_copy(
                src_ref=source(peer),
                dst_ref=target(mine),
                send_sem=send_sem.at[chunk, peer],
                recv_sem=recv_sem.at[chunk, mine],
                device_id=device(peer),
                device_id_type=MESH,
            ).start()

    def wait_all(chunk, count, mine, device, source, target, send_sem, recv_sem):
        pltpu.make_async_copy(source(mine), target(mine), recv_sem.at[chunk, mine]).wait()

        @pl.loop(1, count)
        def _(step):
            peer = lax.rem(mine + step, count)
            pltpu.make_async_remote_copy(
                src_ref=source(peer),
                dst_ref=target(peer),
                send_sem=send_sem.at[chunk, peer],
                recv_sem=recv_sem.at[chunk, peer],
                device_id=device(peer),
                device_id_type=MESH,
            ).wait_recv()

    def wait_sent(chunk, count, mine, device, source, target, send_sem, recv_sem):
        @pl.loop(1, count)
        def _(step):
            peer = lax.rem(mine + step, count)
            pltpu.make_async_remote_copy(
                src_ref=source(peer),
                dst_ref=target(peer),
                send_sem=send_sem.at[chunk, peer],
                recv_sem=recv_sem.at[chunk, peer],
                device_id=device(peer),
                device_id_type=MESH,
            ).wait_send()

    def lon_plan(chunk):
        return (
            chunk,
            lon_count,
            lon,
            lon_device,
            lambda owner: lon_piece(chunk, owner),
            lambda owner: column_piece(columns_in, chunk, owner),
            lon_send,
            lon_recv,
        )

    def mode_plan(chunk):
        return (
            chunk,
            sources,
            my_source,
            mode_device,
            lambda owner: mode_piece(modes_out, chunk, owner),
            lambda owner: mode_piece(modes_in, chunk, owner),
            mode_send,
            mode_recv,
        )

    def back_plan(chunk):
        return (
            chunk,
            sources,
            my_source,
            mode_device,
            lambda owner: mode_piece(back_out, chunk, owner),
            lambda owner: mode_piece(back_in, chunk, owner),
            back_send,
            back_recv,
        )

    def tile_plan(chunk):
        return (
            chunk,
            lon_count,
            lon,
            lon_device,
            lambda owner: column_piece(columns_out, chunk, owner),
            lambda owner: tile_piece(chunk, owner),
            tile_send,
            tile_recv,
        )

    def send_rows_along(part, chunk):
        for group in range(groups):
            peer = group * parts + part
            source = lon_piece(chunk, peer)
            target = column_piece(columns_in, chunk, lon)

            @pl.when(peer == lon)
            def _():
                pltpu.make_async_copy(source, target, lon_recv.at[chunk, lon]).start()

            @pl.when(peer != lon)
            def _():
                pltpu.make_async_remote_copy(
                    src_ref=source,
                    dst_ref=target,
                    send_sem=lon_send.at[chunk, peer],
                    recv_sem=lon_recv.at[chunk, lon],
                    device_id=lon_device(peer),
                    device_id_type=MESH,
                ).start()

    @pl.loop(0, tile_rows // BLOCK_ROWS)
    def _(row_block):
        row = row_block * BLOCK_ROWS
        token = lax.broadcasted_iota(jnp.int32, (block, reach), 0)
        other = lax.broadcasted_iota(jnp.int32, (block, reach), 1)
        top = lat * tile_rows + row
        start = jnp.clip(top + token // BLOCK_COLS - RADIUS, 0, total_rows - span)
        down = top - RADIUS + other // key_cols - start
        across = other % key_cols - near - token % BLOCK_COLS
        inside = (down >= 0) & (down < span) & (across >= -RADIUS) & (across <= RADIUS)
        bias[...] = jnp.where(inside, 0.0, -1e30)

        @pl.loop(0, col_blocks)
        def _(col_block):
            attend(row, pl.multiple_of(col_block * BLOCK_COLS, BLOCK_COLS))

        for index in range(BLOCK_ROWS // chunk_rows):
            ready = row_block * (BLOCK_ROWS // chunk_rows) + index
            send_rows_along(ready // CHUNKS, lax.rem(ready, CHUNKS))

    for chunk in range(CHUNKS):
        wait_all(*lon_plan(chunk))
        first = chunk * chunk_rows
        field = jnp.concatenate([columns_in[first + row] for row in range(chunk_rows)], axis=1)
        along = jnp.dot(forward_ref[...], field, preferred_element_type=jnp.float32)
        along = jnp.concatenate(
            [
                along[:, row * LANES : (row + 1) * LANES].reshape(sources, slots, LANES)
                for row in range(chunk_rows)
            ],
            axis=1,
        )
        modes_out[:, chunk * stretch : (chunk + 1) * stretch, :] = along.astype(jnp.bfloat16)
        send_all(*mode_plan(chunk))
    for chunk in range(CHUNKS):
        wait_all(*mode_plan(chunk))
    modes_work[...] = modes_in[...].astype(jnp.float32).reshape(modes_work.shape)

    batch = 4 if modes % 4 == 0 else modes
    for start in range(0, modes, batch):
        members = range(start, start + batch)

        def every_row(slot):
            return modes_work[pl.ds(slot, total_rows, stride=slots), :].astype(jnp.bfloat16)

        field = jnp.concatenate(
            [
                jnp.concatenate([every_row(2 * mode), every_row(2 * mode + 1)], axis=0)
                for mode in members
            ],
            axis=1,
        )
        spectrum = (
            jnp.dot(lat_forward_ref[...], field, preferred_element_type=jnp.float32) * factor
        )
        spectrum = jnp.concatenate(
            [
                jnp.concatenate(
                    [
                        spectrum[:kept_rows, index * LANES : (index + 1) * LANES],
                        spectrum[kept_rows:, index * LANES : (index + 1) * LANES],
                    ],
                    axis=1,
                )
                for index in range(batch)
            ],
            axis=0,
        ).astype(jnp.bfloat16)
        hidden = jnp.dot(spectrum, weight_one[...], preferred_element_type=jnp.float32)
        hidden = jnp.maximum(hidden + bias_one[...], 0.0).astype(jnp.bfloat16)
        filtered = jnp.dot(hidden, weight_two[...], preferred_element_type=jnp.float32)
        filtered = filtered + bias_two[...]
        filtered = jnp.concatenate(
            [
                jnp.concatenate(
                    [
                        filtered[index * kept_rows : (index + 1) * kept_rows, :LANES],
                        filtered[index * kept_rows : (index + 1) * kept_rows, LANES:],
                    ],
                    axis=0,
                )
                for index in range(batch)
            ],
            axis=1,
        ).astype(jnp.bfloat16)
        rows = jnp.dot(lat_inverse_ref[...], filtered, preferred_element_type=jnp.float32)
        for index, mode in enumerate(members):
            lanes = slice(index * LANES, (index + 1) * LANES)
            modes_work[pl.ds(2 * mode, total_rows, stride=slots), :] = rows[:total_rows, lanes]
            modes_work[pl.ds(2 * mode + 1, total_rows, stride=slots), :] = rows[total_rows:, lanes]
    back_out[...] = modes_work[...].reshape(back_out.shape).astype(jnp.bfloat16)
    for chunk in range(CHUNKS):
        send_all(*back_plan(chunk))
    for chunk in range(CHUNKS):
        wait_all(*back_plan(chunk))
        first = chunk * chunk_rows
        piece = back_in[:, chunk * stretch : (chunk + 1) * stretch, :].astype(jnp.float32)
        field = jnp.concatenate(
            [
                piece[:, row * slots : (row + 1) * slots, :].reshape(sources * slots, LANES)
                for row in range(chunk_rows)
            ],
            axis=1,
        ).astype(jnp.bfloat16)
        whole = jnp.dot(inverse_ref[...], field, preferred_element_type=jnp.float32) * factor
        for row in range(chunk_rows):
            columns_out[first + row] = whole[:, row * LANES : (row + 1) * LANES].astype(
                jnp.bfloat16
            )
        send_all(*tile_plan(chunk))
    for chunk in range(CHUNKS):
        wait_all(*tile_plan(chunk))
    for chunk in range(CHUNKS):
        for plan in (lon_plan, mode_plan, back_plan, tile_plan):
            wait_sent(*plan(chunk))

    @pl.when(has_upper)
    def _():
        for index in (2, 3, 4):
            transfer(index).wait_send()

    @pl.when(has_lower)
    def _():
        for index in (5, 6, 7):
            transfer(index).wait_send()


def shards(
    grid_tokens,
    attention_gain,
    score_weight,
    value_weight,
    output_weight,
    mixer_gain,
    first_weight,
    first_bias,
    second_weight,
    second_bias,
):
    tile_rows, tile_cols, features = grid_tokens.shape
    lat_count = lax.axis_size("lat")
    lon_count = lax.axis_size("lon")
    pairs = features // LANES
    parts = lon_count // pairs
    sources = lat_count * parts
    part_rows = tile_rows // parts
    total_rows = tile_rows * lat_count
    total_cols = tile_cols * lon_count
    modes = total_cols // 4 // sources
    slots = -(-2 * modes // 8) * 8
    tables = mixer_tables(total_rows, total_cols, sources, slots)
    padded_rows = tile_rows + 2 * RADIUS
    block = BLOCK_ROWS * BLOCK_COLS
    reach = (BLOCK_ROWS + 2 * RADIUS) * (BLOCK_COLS + EDGE)
    vmem = pl.BlockSpec(memory_space=pltpu.VMEM)
    shape = jax.ShapeDtypeStruct(grid_tokens.shape, jnp.bfloat16)
    modes_shape = (sources, part_rows * slots, LANES)
    after_attention, mixer_in, spectral = pl.pallas_call(
        functools.partial(block_kernel, lat_count, lon_count),
        out_shape=(shape, shape, shape),
        in_specs=[vmem] * 14,
        out_specs=(vmem, vmem, vmem),
        scratch_shapes=[
            pltpu.VMEM((padded_rows, tile_cols + 2 * EDGE, features), jnp.bfloat16),
            pltpu.VMEM((pairs, tile_rows, tile_cols, LANES), jnp.bfloat16),
            pltpu.VMEM((2 * pairs, padded_rows, tile_cols + EDGE, LANES), jnp.bfloat16),
            pltpu.VMEM((block, reach), jnp.float32),
            pltpu.VMEM((part_rows, total_cols, LANES), jnp.bfloat16),
            pltpu.VMEM(modes_shape, jnp.bfloat16),
            pltpu.VMEM(modes_shape, jnp.bfloat16),
            pltpu.VMEM((sources * part_rows * slots, LANES), jnp.float32),
            pltpu.VMEM(modes_shape, jnp.bfloat16),
            pltpu.VMEM(modes_shape, jnp.bfloat16),
            pltpu.VMEM((part_rows, total_cols, LANES), jnp.bfloat16),
            pltpu.VMEM((2 * LANES, 2 * LANES), jnp.bfloat16),
            pltpu.VMEM((1, 2 * LANES), jnp.float32),
            pltpu.VMEM((2 * LANES, 2 * LANES), jnp.bfloat16),
            pltpu.VMEM((1, 2 * LANES), jnp.float32),
            pltpu.SemaphoreType.DMA((8,)),
            pltpu.SemaphoreType.DMA((8,)),
            pltpu.SemaphoreType.DMA,
        ]
        + [
            pltpu.SemaphoreType.DMA((CHUNKS, count))
            for count in (lon_count, sources, sources, lon_count)
            for _ in range(2)
        ],
        compiler_params=pltpu.CompilerParams(
            collective_id=1, has_side_effects=True, vmem_limit_bytes=56 * 1024 * 1024
        ),
        name="mixed_block",
    )(
        grid_tokens,
        attention_gain.reshape(1, features),
        score_weight,
        value_weight,
        output_weight,
        mixer_gain.reshape(1, features),
        *tables,
        first_weight,
        first_bias,
        second_weight,
        second_bias,
    )
    summed = (
        after_attention.astype(jnp.float32)
        + mixer_in.astype(jnp.float32)
        + spectral.astype(jnp.float32)
    )
    return summed.astype(jnp.bfloat16)


def solution(mesh):
    placed = (P("lat", "lon", None), P(), P(), P(), P(), P(), P(), P(), P(), P())
    return jax.shard_map(
        shards, mesh=mesh, in_specs=placed, out_specs=P("lat", "lon", None), check_vma=False
    )
```

```python
import functools
import math

import jax
import jax.numpy as jnp
import numpy as np
from jax import lax
from jax.experimental import pallas as pl
from jax.experimental.pallas import tpu as pltpu
from jax.sharding import PartitionSpec as P

HEADS = 8
RADIUS = 6


LANES = 128
CHUNKS = 3
MESH = pl.DeviceIdType.MESH
BLOCK_ROWS = 8
BLOCK_COLS = 16
EDGE = 16


def mixer_tables(total_rows, total_cols, sources, slots):
    kept_rows = total_rows // 2
    kept_cols = total_cols // 4
    modes = kept_cols // sources
    column = np.arange(total_cols)
    angle = 2.0 * np.pi * (np.outer(np.arange(kept_cols), column) % total_cols) / total_cols
    cosine = np.cos(angle).reshape(sources, modes, total_cols)
    sine = np.sin(angle).reshape(sources, modes, total_cols)
    forward = np.zeros((sources, slots, total_cols))
    forward[:, 0 : 2 * modes : 2] = cosine
    forward[:, 1 : 2 * modes : 2] = -sine
    doubled = np.full((kept_cols, 1), 2.0)
    doubled[0] = 1.0
    inverse = (forward.reshape(sources, slots, total_cols)).copy()
    inverse[:, 0 : 2 * modes : 2] *= doubled.reshape(sources, modes, 1)
    inverse[:, 1 : 2 * modes : 2] *= doubled.reshape(sources, modes, 1)
    forward = forward.reshape(sources * slots, total_cols)
    inverse = inverse.reshape(sources * slots, total_cols).T
    frequency = np.arange(kept_rows)
    frequency = frequency + np.where(frequency >= kept_rows // 2, total_rows - kept_rows, 0)
    angle = 2.0 * np.pi * (np.outer(frequency, np.arange(total_rows)) % total_rows) / total_rows
    cosine = np.cos(angle)
    sine = np.sin(angle)
    lat_forward = np.block([[cosine, sine], [-sine, cosine]])
    lat_inverse = np.block([[cosine.T, -sine.T], [sine.T, cosine.T]])
    return tuple(
        np.asarray(table, dtype=jnp.bfloat16)
        for table in (forward, lat_forward, lat_inverse, inverse)
    )


def paired_weights(weight_ref, bias_ref, group, joined, offset):
    size = weight_ref.shape[2]
    blocks = LANES // size
    for index in range(blocks):
        source = group * blocks + index

        def wide(values):
            blank = jnp.zeros_like(values)
            return [values if place == index else blank for place in range(blocks)]

        real = weight_ref[0, source]
        imag = weight_ref[1, source]
        lower = index * size
        joined[lower : lower + size, :] = jnp.concatenate(
            wide(real) + wide(imag), axis=1
        ).astype(jnp.bfloat16)
        lower = LANES + index * size
        joined[lower : lower + size, :] = jnp.concatenate(
            wide(-imag) + wide(real), axis=1
        ).astype(jnp.bfloat16)
    offset[...] = jnp.concatenate(
        [
            bias_ref[part, pl.ds(group * blocks + index, 1), :]
            for part in range(2)
            for index in range(blocks)
        ],
        axis=1,
    )


def block_kernel(
    lat_count,
    lon_count,
    token_ref,
    gain_ref,
    score_ref,
    value_ref,
    output_ref,
    mixer_gain_ref,
    forward_ref,
    lat_forward_ref,
    lat_inverse_ref,
    inverse_ref,
    first_weight_ref,
    first_bias_ref,
    second_weight_ref,
    second_bias_ref,
    sum_ref,
    after_ref,
    mixer_ref,
    spectral_ref,
    padded,
    query,
    key_value,
    bias,
    columns_in,
    modes_out,
    modes_in,
    modes_work,
    back_out,
    back_in,
    columns_out,
    weight_one,
    bias_one,
    weight_two,
    bias_two,
    send_sem,
    recv_sem,
    own_sem,
    lon_send,
    lon_recv,
    mode_send,
    mode_recv,
    back_send,
    back_recv,
    tile_send,
    tile_recv,
):
    tile_rows, tile_cols, features = token_ref.shape
    total_rows = tile_rows * lat_count
    span = 2 * RADIUS + 1
    head_size = features // HEADS
    pairs = features // LANES
    lat = lax.axis_index("lat")
    lon = lax.axis_index("lon")
    has_upper = lat > 0
    has_lower = lat < lat_count - 1
    left = lax.rem(lon + lon_count - 1, lon_count)
    right = lax.rem(lon + 1, lon_count)

    groups = features // LANES
    parts = lon_count // groups
    sources = lat_count * parts
    part_rows = tile_rows // parts
    chunk_rows = part_rows // CHUNKS
    total_cols = tile_cols * lon_count
    kept_rows = total_rows // 2
    modes = total_cols // 4 // sources
    slots = modes_in.shape[1] // part_rows
    stretch = chunk_rows * slots
    factor = 1.0 / math.sqrt(total_rows * total_cols)
    my_group = lon // parts
    my_part = lax.rem(lon, parts)
    my_source = lat * parts + my_part

    def lon_device(index):
        return (lat, index)

    def mode_device(index):
        return (index // parts, my_group * parts + lax.rem(index, parts))

    send_rows = {-1: (0, RADIUS), 0: (0, tile_rows), 1: (tile_rows - RADIUS, RADIUS)}
    land_rows = {
        -1: (tile_rows + RADIUS, RADIUS),
        0: (RADIUS, tile_rows),
        1: (0, RADIUS),
    }
    send_cols = {-1: (0, EDGE), 0: (0, tile_cols), 1: (tile_cols - EDGE, EDGE)}
    land_cols = {-1: (tile_cols + EDGE, EDGE), 0: (EDGE, tile_cols), 1: (0, EDGE)}
    moves = [(0, -1), (0, 1)] + [(down, across) for down in (-1, 1) for across in (0, -1, 1)]

    def transfer(index):
        down, across = moves[index]
        target = {-1: left, 0: lon, 1: right}[across]
        return pltpu.make_async_remote_copy(
            src_ref=token_ref.at[pl.ds(*send_rows[down]), pl.ds(*send_cols[across]), :],
            dst_ref=padded.at[pl.ds(*land_rows[down]), pl.ds(*land_cols[across]), :],
            send_sem=send_sem.at[index],
            recv_sem=recv_sem.at[index],
            device_id=(lat + down, target),
            device_id_type=MESH,
        )

    barrier = pltpu.get_barrier_semaphore()

    def greet(row):
        for column in (left, lon, right):
            pl.semaphore_signal(
                barrier, inc=1, device_id=(row, column), device_id_type=MESH
            )

    for column in (left, right):
        pl.semaphore_signal(barrier, inc=1, device_id=(lat, column), device_id_type=MESH)

    @pl.loop(1, lon_count)
    def _(step):
        pl.semaphore_signal(
            barrier,
            inc=1,
            device_id=lon_device(lax.rem(lon + step, lon_count)),
            device_id_type=MESH,
        )

    @pl.loop(1, sources)
    def _(step):
        pl.semaphore_signal(
            barrier,
            inc=1,
            device_id=mode_device(lax.rem(my_source + step, sources)),
            device_id_type=MESH,
        )

    @pl.when(has_upper)
    def _():
        greet(lat - 1)

    @pl.when(has_lower)
    def _():
        greet(lat + 1)

    above = (lat + lat_count - 1) // lat_count
    below = (2 * lat_count - 2 - lat) // lat_count
    pl.semaphore_wait(barrier, lon_count + sources + 3 * (above + below))

    for index in (0, 1):
        transfer(index).start()

    @pl.when(has_upper)
    def _():
        for index in (2, 3, 4):
            transfer(index).start()

    @pl.when(has_lower)
    def _():
        for index in (5, 6, 7):
            transfer(index).start()

    own = pltpu.make_async_copy(
        token_ref,
        padded.at[pl.ds(RADIUS, tile_rows), pl.ds(EDGE, tile_cols), :],
        own_sem,
    )
    own.start()
    blank = jnp.zeros((RADIUS, tile_cols + 2 * EDGE, features), jnp.bfloat16)

    @pl.when(jnp.logical_not(has_upper))
    def _():
        padded[:RADIUS] = blank

    @pl.when(jnp.logical_not(has_lower))
    def _():
        padded[tile_rows + RADIUS :] = blank

    def norm(data, gain):
        centre = jnp.mean(data, axis=-1, keepdims=True)
        centred = data - centre
        spread = jnp.mean(centred * centred, axis=-1, keepdims=True)
        return (centred * lax.rsqrt(spread + 1e-05) * gain).astype(jnp.bfloat16)

    def spread_pairs(ref, base, rows, values, cols):
        shaped = values.astype(jnp.bfloat16).reshape(RADIUS, cols, values.shape[1])
        for pair in range(values.shape[1] // LANES):
            ref[base + pair, rows] = shaped[:, :, pair * LANES : (pair + 1) * LANES]

    scale = 1.0 / math.sqrt(head_size)

    @pl.loop(0, tile_rows // RADIUS)
    def _(step):
        rows = pl.ds(step * RADIUS, RADIUS)
        data = token_ref[rows].astype(jnp.float32).reshape(-1, features)
        inputs = norm(data, gain_ref[...])
        values = jnp.dot(inputs, score_ref[:, :features], preferred_element_type=jnp.float32)
        values = values.astype(jnp.bfloat16).astype(jnp.float32) * scale
        spread_pairs(query, 0, rows, values, tile_cols)

    paired_weights(first_weight_ref, first_bias_ref, my_group, weight_one, bias_one)
    paired_weights(second_weight_ref, second_bias_ref, my_group, weight_two, bias_two)
    own.wait()
    for index in (0, 1):
        transfer(index).wait()

    @pl.when(has_lower)
    def _():
        for index in (2, 3, 4):
            transfer(index).wait_recv()

    @pl.when(has_upper)
    def _():
        for index in (5, 6, 7):
            transfer(index).wait_recv()

    near = EDGE // 2
    wide = tile_cols + 2 * near

    @pl.loop(0, tile_rows // RADIUS + 2)
    def _(step):
        rows = pl.ds(step * RADIUS, RADIUS)
        data = padded[rows].astype(jnp.float32)[:, near : near + wide, :].reshape(-1, features)
        inputs = norm(data, gain_ref[...])
        keys = jnp.dot(inputs, score_ref[:, features:], preferred_element_type=jnp.float32)
        spread_pairs(key_value, 0, rows, keys, wide)
        values = jnp.dot(inputs, value_ref[...], preferred_element_type=jnp.float32)
        spread_pairs(key_value, pairs, rows, values, wide)

    block = BLOCK_ROWS * BLOCK_COLS
    key_rows = BLOCK_ROWS + 2 * RADIUS
    key_cols = BLOCK_COLS + 2 * near
    reach = key_rows * key_cols
    col_blocks = tile_cols // BLOCK_COLS

    def attend(row, col):
        lower_lane = lax.broadcasted_iota(jnp.int32, (block, LANES), 1) < head_size
        heads = []
        for pair in range(pairs):
            asked = query[pair, pl.ds(row, BLOCK_ROWS), pl.ds(col, BLOCK_COLS), :]
            asked = asked.reshape(block, LANES).astype(jnp.float32)
            asked = jnp.concatenate(
                [jnp.where(lower_lane, asked, 0.0), jnp.where(lower_lane, 0.0, asked)], axis=0
            ).astype(jnp.bfloat16)
            window = (pl.ds(row, key_rows), pl.ds(col, key_cols), slice(None))
            keys = key_value[(pair, *window)].reshape(reach, LANES)
            values = key_value[(pairs + pair, *window)].reshape(reach, LANES)
            scores = lax.dot_general(
                asked, keys, (((1,), (1,)), ((), ())), preferred_element_type=jnp.float32
            )
            scores = (scores.reshape(2, block, reach) + bias[...]).reshape(2 * block, reach)
            weights = jnp.exp(scores - jnp.max(scores, axis=1, keepdims=True))
            total = jnp.sum(weights, axis=1, keepdims=True)
            mixed = jnp.dot(
                weights.astype(jnp.bfloat16), values, preferred_element_type=jnp.float32
            )
            mixed = mixed / total
            heads.append(jnp.where(lower_lane, mixed[:block], mixed[block:]))
        attended = jnp.concatenate(heads, axis=1).astype(jnp.bfloat16)
        place = (pl.ds(row, BLOCK_ROWS), pl.ds(col, BLOCK_COLS), slice(None))
        after = token_ref[place].astype(jnp.float32).reshape(block, features)
        after = after + jnp.dot(attended, output_ref[...], preferred_element_type=jnp.float32)
        after = after.astype(jnp.bfloat16)
        shape = (BLOCK_ROWS, BLOCK_COLS, features)
        after_ref[place] = after.reshape(shape)
        mixer_ref[place] = norm(after.astype(jnp.float32), mixer_gain_ref[...]).reshape(shape)

    def lon_piece(chunk, owner):
        group = owner // parts
        part = lax.rem(owner, parts)
        return mixer_ref.at[
            pl.ds(part * part_rows + chunk * chunk_rows, chunk_rows),
            :,
            pl.ds(pl.multiple_of(group * LANES, LANES), LANES),
        ]

    def column_piece(ref, chunk, owner):
        return ref.at[
            pl.ds(chunk * chunk_rows, chunk_rows),
            pl.ds(pl.multiple_of(owner * tile_cols, 16), tile_cols),
            :,
        ]

    def mode_piece(ref, chunk, owner):
        return ref.at[owner, pl.ds(chunk * stretch, stretch), :]

    def tile_piece(chunk, owner):
        group = owner // parts
        part = lax.rem(owner, parts)
        return spectral_ref.at[
            pl.ds(part * part_rows + chunk * chunk_rows, chunk_rows),
            :,
            pl.ds(pl.multiple_of(group * LANES, LANES), LANES),
        ]

    def send_all(chunk, count, mine, device, source, target, send_sem, recv_sem):
        pltpu.make_async_copy(source(mine), target(mine), recv_sem.at[chunk, mine]).start()

        @pl.loop(1, count)
        def _(step):
            peer = lax.rem(mine + step, count)
            pltpu.make_async_remote_copy(
                src_ref=source(peer),
                dst_ref=target(mine),
                send_sem=send_sem.at[chunk, peer],
                recv_sem=recv_sem.at[chunk, mine],
                device_id=device(peer),
                device_id_type=MESH,
            ).start()

    def wait_all(chunk, count, mine, device, source, target, send_sem, recv_sem):
        pltpu.make_async_copy(source(mine), target(mine), recv_sem.at[chunk, mine]).wait()

        @pl.loop(1, count)
        def _(step):
            peer = lax.rem(mine + step, count)
            pltpu.make_async_remote_copy(
                src_ref=source(peer),
                dst_ref=target(peer),
                send_sem=send_sem.at[chunk, peer],
                recv_sem=recv_sem.at[chunk, peer],
                device_id=device(peer),
                device_id_type=MESH,
            ).wait_recv()

    def wait_sent(chunk, count, mine, device, source, target, send_sem, recv_sem):
        @pl.loop(1, count)
        def _(step):
            peer = lax.rem(mine + step, count)
            pltpu.make_async_remote_copy(
                src_ref=source(peer),
                dst_ref=target(peer),
                send_sem=send_sem.at[chunk, peer],
                recv_sem=recv_sem.at[chunk, peer],
                device_id=device(peer),
                device_id_type=MESH,
            ).wait_send()

    def lon_plan(chunk):
        return (
            chunk,
            lon_count,
            lon,
            lon_device,
            lambda owner: lon_piece(chunk, owner),
            lambda owner: column_piece(columns_in, chunk, owner),
            lon_send,
            lon_recv,
        )

    def mode_plan(chunk):
        return (
            chunk,
            sources,
            my_source,
            mode_device,
            lambda owner: mode_piece(modes_out, chunk, owner),
            lambda owner: mode_piece(modes_in, chunk, owner),
            mode_send,
            mode_recv,
        )

    def back_plan(chunk):
        return (
            chunk,
            sources,
            my_source,
            mode_device,
            lambda owner: mode_piece(back_out, chunk, owner),
            lambda owner: mode_piece(back_in, chunk, owner),
            back_send,
            back_recv,
        )

    def tile_plan(chunk):
        return (
            chunk,
            lon_count,
            lon,
            lon_device,
            lambda owner: column_piece(columns_out, chunk, owner),
            lambda owner: tile_piece(chunk, owner),
            tile_send,
            tile_recv,
        )

    def send_rows_along(part, chunk):
        for group in range(groups):
            peer = group * parts + part
            source = lon_piece(chunk, peer)
            target = column_piece(columns_in, chunk, lon)

            @pl.when(peer == lon)
            def _():
                pltpu.make_async_copy(source, target, lon_recv.at[chunk, lon]).start()

            @pl.when(peer != lon)
            def _():
                pltpu.make_async_remote_copy(
                    src_ref=source,
                    dst_ref=target,
                    send_sem=lon_send.at[chunk, peer],
                    recv_sem=lon_recv.at[chunk, lon],
                    device_id=lon_device(peer),
                    device_id_type=MESH,
                ).start()

    @pl.loop(0, tile_rows // BLOCK_ROWS)
    def _(row_block):
        row = row_block * BLOCK_ROWS
        token = lax.broadcasted_iota(jnp.int32, (block, reach), 0)
        other = lax.broadcasted_iota(jnp.int32, (block, reach), 1)
        top = lat * tile_rows + row
        start = jnp.clip(top + token // BLOCK_COLS - RADIUS, 0, total_rows - span)
        down = top - RADIUS + other // key_cols - start
        across = other % key_cols - near - token % BLOCK_COLS
        inside = (down >= 0) & (down < span) & (across >= -RADIUS) & (across <= RADIUS)
        bias[...] = jnp.where(inside, 0.0, -1e30)

        @pl.loop(0, col_blocks)
        def _(col_block):
            attend(row, pl.multiple_of(col_block * BLOCK_COLS, BLOCK_COLS))

        for index in range(BLOCK_ROWS // chunk_rows):
            ready = row_block * (BLOCK_ROWS // chunk_rows) + index
            send_rows_along(ready // CHUNKS, lax.rem(ready, CHUNKS))

    for chunk in range(CHUNKS):
        wait_all(*lon_plan(chunk))
        first = chunk * chunk_rows
        field = jnp.concatenate([columns_in[first + row] for row in range(chunk_rows)], axis=1)
        along = jnp.dot(forward_ref[...], field, preferred_element_type=jnp.float32)
        along = jnp.concatenate(
            [
                along[:, row * LANES : (row + 1) * LANES].reshape(sources, slots, LANES)
                for row in range(chunk_rows)
            ],
            axis=1,
        )
        modes_out[:, chunk * stretch : (chunk + 1) * stretch, :] = along.astype(jnp.bfloat16)
        send_all(*mode_plan(chunk))
    for chunk in range(CHUNKS):
        wait_all(*mode_plan(chunk))
    modes_work[...] = modes_in[...].astype(jnp.float32).reshape(modes_work.shape)

    batch = 4 if modes % 4 == 0 else modes
    for start in range(0, modes, batch):
        members = range(start, start + batch)

        def every_row(slot):
            return modes_work[pl.ds(slot, total_rows, stride=slots), :].astype(jnp.bfloat16)

        field = jnp.concatenate(
            [
                jnp.concatenate([every_row(2 * mode), every_row(2 * mode + 1)], axis=0)
                for mode in members
            ],
            axis=1,
        )
        spectrum = (
            jnp.dot(lat_forward_ref[...], field, preferred_element_type=jnp.float32) * factor
        )
        spectrum = jnp.concatenate(
            [
                jnp.concatenate(
                    [
                        spectrum[:kept_rows, index * LANES : (index + 1) * LANES],
                        spectrum[kept_rows:, index * LANES : (index + 1) * LANES],
                    ],
                    axis=1,
                )
                for index in range(batch)
            ],
            axis=0,
        ).astype(jnp.bfloat16)
        hidden = jnp.dot(spectrum, weight_one[...], preferred_element_type=jnp.float32)
        hidden = jnp.maximum(hidden + bias_one[...], 0.0).astype(jnp.bfloat16)
        filtered = jnp.dot(hidden, weight_two[...], preferred_element_type=jnp.float32)
        filtered = filtered + bias_two[...]
        filtered = jnp.concatenate(
            [
                jnp.concatenate(
                    [
                        filtered[index * kept_rows : (index + 1) * kept_rows, :LANES],
                        filtered[index * kept_rows : (index + 1) * kept_rows, LANES:],
                    ],
                    axis=0,
                )
                for index in range(batch)
            ],
            axis=1,
        ).astype(jnp.bfloat16)
        rows = jnp.dot(lat_inverse_ref[...], filtered, preferred_element_type=jnp.float32)
        for index, mode in enumerate(members):
            lanes = slice(index * LANES, (index + 1) * LANES)
            modes_work[pl.ds(2 * mode, total_rows, stride=slots), :] = rows[:total_rows, lanes]
            modes_work[pl.ds(2 * mode + 1, total_rows, stride=slots), :] = rows[total_rows:, lanes]
    back_out[...] = modes_work[...].reshape(back_out.shape).astype(jnp.bfloat16)
    for chunk in range(CHUNKS):
        send_all(*back_plan(chunk))
    for chunk in range(CHUNKS):
        wait_all(*back_plan(chunk))
        first = chunk * chunk_rows
        piece = back_in[:, chunk * stretch : (chunk + 1) * stretch, :].astype(jnp.float32)
        field = jnp.concatenate(
            [
                piece[:, row * slots : (row + 1) * slots, :].reshape(sources * slots, LANES)
                for row in range(chunk_rows)
            ],
            axis=1,
        ).astype(jnp.bfloat16)
        whole = jnp.dot(inverse_ref[...], field, preferred_element_type=jnp.float32) * factor
        for row in range(chunk_rows):
            columns_out[first + row] = whole[:, row * LANES : (row + 1) * LANES].astype(
                jnp.bfloat16
            )
        send_all(*tile_plan(chunk))
    for chunk in range(CHUNKS):
        wait_all(*tile_plan(chunk))
        for part in range(parts):
            first = part * part_rows + chunk * chunk_rows
            rows = slice(first, first + chunk_rows)
            summed = after_ref[rows].astype(jnp.float32) + mixer_ref[rows].astype(jnp.float32)
            summed = summed + spectral_ref[rows].astype(jnp.float32)
            sum_ref[rows] = summed.astype(jnp.bfloat16)
    for chunk in range(CHUNKS):
        for plan in (lon_plan, mode_plan, back_plan, tile_plan):
            wait_sent(*plan(chunk))

    @pl.when(has_upper)
    def _():
        for index in (2, 3, 4):
            transfer(index).wait_send()

    @pl.when(has_lower)
    def _():
        for index in (5, 6, 7):
            transfer(index).wait_send()


def shards(
    grid_tokens,
    attention_gain,
    score_weight,
    value_weight,
    output_weight,
    mixer_gain,
    first_weight,
    first_bias,
    second_weight,
    second_bias,
):
    tile_rows, tile_cols, features = grid_tokens.shape
    lat_count = lax.axis_size("lat")
    lon_count = lax.axis_size("lon")
    pairs = features // LANES
    parts = lon_count // pairs
    sources = lat_count * parts
    part_rows = tile_rows // parts
    total_rows = tile_rows * lat_count
    total_cols = tile_cols * lon_count
    modes = total_cols // 4 // sources
    slots = -(-2 * modes // 8) * 8
    tables = mixer_tables(total_rows, total_cols, sources, slots)
    padded_rows = tile_rows + 2 * RADIUS
    block = BLOCK_ROWS * BLOCK_COLS
    reach = (BLOCK_ROWS + 2 * RADIUS) * (BLOCK_COLS + EDGE)
    vmem = pl.BlockSpec(memory_space=pltpu.VMEM)
    shape = jax.ShapeDtypeStruct(grid_tokens.shape, jnp.bfloat16)
    modes_shape = (sources, part_rows * slots, LANES)
    return pl.pallas_call(
        functools.partial(block_kernel, lat_count, lon_count),
        out_shape=shape,
        in_specs=[vmem] * 14,
        out_specs=vmem,
        scratch_shapes=[pltpu.VMEM(grid_tokens.shape, jnp.bfloat16) for _ in range(3)]
        + [
            pltpu.VMEM((padded_rows, tile_cols + 2 * EDGE, features), jnp.bfloat16),
            pltpu.VMEM((pairs, tile_rows, tile_cols, LANES), jnp.bfloat16),
            pltpu.VMEM((2 * pairs, padded_rows, tile_cols + EDGE, LANES), jnp.bfloat16),
            pltpu.VMEM((block, reach), jnp.float32),
            pltpu.VMEM((part_rows, total_cols, LANES), jnp.bfloat16),
            pltpu.VMEM(modes_shape, jnp.bfloat16),
            pltpu.VMEM(modes_shape, jnp.bfloat16),
            pltpu.VMEM((sources * part_rows * slots, LANES), jnp.float32),
            pltpu.VMEM(modes_shape, jnp.bfloat16),
            pltpu.VMEM(modes_shape, jnp.bfloat16),
            pltpu.VMEM((part_rows, total_cols, LANES), jnp.bfloat16),
            pltpu.VMEM((2 * LANES, 2 * LANES), jnp.bfloat16),
            pltpu.VMEM((1, 2 * LANES), jnp.float32),
            pltpu.VMEM((2 * LANES, 2 * LANES), jnp.bfloat16),
            pltpu.VMEM((1, 2 * LANES), jnp.float32),
            pltpu.SemaphoreType.DMA((8,)),
            pltpu.SemaphoreType.DMA((8,)),
            pltpu.SemaphoreType.DMA,
        ]
        + [
            pltpu.SemaphoreType.DMA((CHUNKS, count))
            for count in (lon_count, sources, sources, lon_count)
            for _ in range(2)
        ],
        compiler_params=pltpu.CompilerParams(
            collective_id=1, has_side_effects=True, vmem_limit_bytes=56 * 1024 * 1024
        ),
        name="mixed_block",
    )(
        grid_tokens,
        attention_gain.reshape(1, features),
        score_weight,
        value_weight,
        output_weight,
        mixer_gain.reshape(1, features),
        *tables,
        first_weight,
        first_bias,
        second_weight,
        second_bias,
    )


def solution(mesh):
    placed = (P("lat", "lon", None), P(), P(), P(), P(), P(), P(), P(), P(), P())
    return jax.shard_map(
        shards, mesh=mesh, in_specs=placed, out_specs=P("lat", "lon", None), check_vma=False
    )
```
